512 devices in a mesh: seq: 64 (over x, z), chan: 8 (over y, core).
Axes of the slice: x: 4, y: 4, z: 16, core: 2. Of those that a mesh axis runs over, the one named last changes fastest.
Arguments:
- signal: bfloat16 [16384, 8192], P('seq', 'chan'), parts along dimension 1, may hold values from -6 to 6
- cotangent: bfloat16 [16384, 8192], P('seq', 'chan'), parts along dimension 1, may hold values from -6 to 6
- decay_rate: float32 [16, 8192], P(None, 'chan'), parts along dimension 1, may hold values from 1.2207031e-05 to 0.0333333333
- residue: float32 [16, 8192], P(None, 'chan'), parts along dimension 1, may hold values from -1.5 to 1.5
- skip_gain: float32 [8192], P('chan'), parts along dimension 0, may hold values from 0.5 to 1.5
Outputs:
- output: bfloat16 [16384, 8192], P('seq', 'chan'), parts along dimension 1
- grad_signal: bfloat16 [16384, 8192], P('seq', 'chan'), parts along dimension 1
The draws below stay inside these ranges and needn't reach their ends.
There are 8 independent parts, one for each index of `chan`. The reference program is written for one: setup_inputs(seed, part) draws one part's arguments, and reference() takes and returns one part's arrays. A program takes and returns all parts, laid end to end along the dimension named above; each array names one. Nothing has to cross between parts.
All inputs are finite; a program needn't handle non-finite values.
Results may differ from the reference program's by a relative error of at most 0.007.
Values sent between devices are 32-bit elements; how exact they have to be, the bound alone decides.
No kernel may reach another device: no remote copies, remote signals or barrier semaphores. Data moves between devices by JAX's collectives and lax.ppermute only.
A program may use at most 128 MiB of HBM per device.

```python
import math
import jax
import jax.numpy as jnp
from jax import lax

CH = 1024
NS = 16
BLOCK = 32
TOKENS = 16384


def draw_decay_rate(key, part):
    first_key, second_key, third_key = jax.random.split(key, 3)
    slow_share = 0.5
    is_slow = jax.random.uniform(first_key, (NS, CH), jnp.float32) < slow_share
    slow_fraction = jax.random.uniform(second_key, (NS, CH), jnp.float32)
    fast_fraction = jax.random.uniform(third_key, (NS, CH), jnp.float32)
    slow_rates = jnp.exp(math.log(0.2 / TOKENS) + slow_fraction * math.log(10.0))
    fast_rates = jnp.exp(math.log(1.0 / 400.0) + fast_fraction * math.log(400.0 / 30.0))
    rates = jnp.where(is_slow, slow_rates, fast_rates)
    return jnp.clip(rates, 0.2 / TOKENS, 1.0 / 30).astype(jnp.float32)


def block_scale(own_key, dims, shards, least, largest):
    level = 1.0
    for position, parts in shards:
        steps = jax.random.uniform(jax.random.fold_in(jax.random.fold_in(own_key, 6), position), (parts,), jnp.float32, least / len(shards), largest / len(shards))
        level = level * jnp.repeat(jnp.exp(steps), dims[position] // parts).reshape((-1,) + (1,) * (len(dims) - 1 - position))
    return level


def gaussian(key, extent, spread, limit, pieces=(), kind=jnp.bfloat16):
    result = spread * jax.random.normal(key, extent, jnp.float32)
    if pieces:
        result = result * block_scale(key, extent, pieces, -0.22, 0.18)
    return jnp.clip(result, -limit, limit).astype(kind)


def setup_inputs(seed: int = 0, part: int = 0) -> dict:
    arg_keys = jax.random.split(jax.random.key(seed), 6)
    part_keys = jax.random.split(jax.random.fold_in(arg_keys[5], part), 6)
    return {
        "signal": gaussian(part_keys[0], (TOKENS, CH), 1.0, 6.0, ((0, 64),)),
        "cotangent": gaussian(part_keys[1], (TOKENS, CH), 1.0, 6.0, ((0, 64),)),
        "decay_rate": draw_decay_rate(jax.random.fold_in(jax.random.fold_in(arg_keys[5], part), 71), part),
        "residue": gaussian(part_keys[3], (NS, CH), NS ** -0.5, 1.5, (), jnp.float32),
        "skip_gain": jnp.clip(jax.random.uniform(part_keys[4], (CH,), jnp.float32, 0.5, 1.5), 0.5, 1.5),
    }


def build_tables(decay_rate, residue, block_rows):
    positions = jnp.arange(block_rows, dtype=jnp.float32)
    weight = residue * jnp.sqrt(-jnp.expm1(-2.0 * decay_rate))
    decays = jnp.exp(-decay_rate[:, None, :] * positions[None, :, None])
    filter_taps = lax.optimization_barrier(jnp.sum(weight[:, None, :] * decays, axis=0))
    lag_index = jnp.arange(block_rows, dtype=jnp.int32)[:, None] - jnp.arange(block_rows, dtype=jnp.int32)[None, :]
    picked = jnp.take(filter_taps, jnp.clip(lag_index, 0, block_rows - 1).astype(jnp.int32), axis=0)
    toeplitz = jnp.where((lag_index >= 0)[:, :, None], picked, jnp.float32(0.0))
    tail_decay = jnp.flip(decays, axis=1)
    readout = weight[:, None, :] * jnp.exp(-decay_rate[:, None, :] * (positions + 1.0)[None, :, None])
    return (toeplitz, tail_decay, readout)

def convolve(signal, decay_rate, residue, skip_gain):
    channels = signal.shape[1]
    toeplitz, tail_decay, readout = build_tables(decay_rate, residue, BLOCK)
    blocks = signal.astype(jnp.float32).reshape(-1, BLOCK, channels)
    within = jnp.einsum('tsc,bsc->btc', toeplitz, blocks, precision=lax.Precision.HIGHEST)
    block_ends = jnp.einsum('nsc,bsc->bnc', tail_decay, blocks, precision=lax.Precision.HIGHEST)
    block_decay = jnp.exp(-decay_rate * BLOCK)

    def advance(state_now, block_end):
        return (block_decay * state_now + block_end, state_now)
    _, entering = lax.scan(advance, jnp.zeros(decay_rate.shape, jnp.float32), block_ends)
    carried = jnp.einsum('ntc,bnc->btc', readout, entering, precision=lax.Precision.HIGHEST)
    total = within + carried + skip_gain[None, None, :] * blocks
    return total.reshape(-1, channels).astype(jnp.bfloat16)

def reference(signal, cotangent, decay_rate, residue, skip_gain):
    output = convolve(signal, decay_rate, residue, skip_gain)
    grad_signal = jnp.flip(convolve(jnp.flip(cotangent, 0), decay_rate, residue, skip_gain), 0)
    return (output, grad_signal)
```

```python
import functools
import jax
import jax.numpy as jnp
from jax import lax
from jax.experimental import pallas as pl
from jax.experimental.pallas import tpu as pltpu
from jax.sharding import PartitionSpec as P

SUB = 8
LANES = 128
F32 = jnp.float32


def row_of(table, n):
    return jnp.broadcast_to(table[n : n + 1, :], (SUB, LANES))


def block_index():
    return lax.broadcasted_iota(jnp.int32, (SUB, LANES), 0)


def blocked_position(x_ref, r, length):
    return x_ref[pl.ds(r, SUB, stride=length), :]


def block_ends(x_ref, decay, order, length):
    ends = [None] * len(decay)
    for step, r in enumerate(order):
        x = blocked_position(x_ref, r, length)
        for n in range(len(decay)):
            ends[n] = x if step == 0 else decay[n] * ends[n] + x
    return ends


def orders(length):
    return list(range(length)), list(range(length - 1, -1, -1))


def ends_kernel(signal_ref, cotangent_ref, rate_ref, ends_ref, span_ref, x_ref, g_ref):
    positions = signal_ref.shape[0]
    length = positions // SUB
    states = rate_ref.shape[0]
    x_ref[...] = signal_ref[...].astype(F32)
    g_ref[...] = cotangent_ref[...].astype(F32)
    rate = rate_ref[...]
    span_ref[...] = jnp.exp(-rate * float(positions))
    decay_table = jnp.exp(-rate)
    decay = [row_of(decay_table, n) for n in range(states)]
    block = block_index()
    forward, backward = orders(length)
    later = (length * (SUB - 1 - block)).astype(F32)
    earlier = (length * block).astype(F32)
    for side, (ref, order, distance) in enumerate(
        ((x_ref, forward, later), (g_ref, backward, earlier))
    ):
        ends = block_ends(ref, decay, order, length)
        for n in range(states):
            scaled = jnp.exp(-row_of(rate, n) * distance) * ends[n]
            ends_ref[side, n : n + 1, :] = jnp.sum(scaled, axis=0, keepdims=True)


def entering_states(ends, rate, length, forward):
    block = block_index()
    entering = []
    for n in range(len(ends)):
        total = ends[n]
        reach = 1
        while reach < SUB:
            ratio = jnp.exp(-row_of(rate, n) * float(length * reach))
            total = total + ratio * shifted_blocks(total, reach, block, forward)
            reach *= 2
        entering.append(shifted_blocks(total, 1, block, forward))
    return entering


def shifted_blocks(x, by, block, forward):
    if forward:
        return jnp.where(block >= by, pltpu.roll(x, by, 0), 0.0)
    return jnp.where(block < SUB - by, pltpu.roll(x, SUB - by, 0), 0.0)


def within_kernel(
    signal_ref, cotangent_ref, rate_ref, weight_ref, gain_ref, y_ref, z_ref, x_ref, g_ref
):
    positions = signal_ref.shape[0]
    length = positions // SUB
    states = rate_ref.shape[0]
    x_ref[...] = signal_ref[...].astype(F32)
    g_ref[...] = cotangent_ref[...].astype(F32)
    rate = rate_ref[...]
    decay_table = jnp.exp(-rate)
    decay = [row_of(decay_table, n) for n in range(states)]
    weight_table = weight_ref[...]
    weight = [row_of(weight_table, n) for n in range(states)]
    gain = jnp.broadcast_to(gain_ref[...], (SUB, LANES))
    forward, backward = orders(length)
    for ref, out_ref, order in ((x_ref, y_ref, forward), (g_ref, z_ref, backward)):
        ends = block_ends(ref, decay, order, length)
        state = entering_states(ends, rate, length, order[0] == 0)
        for r in order:
            x = blocked_position(ref, r, length)
            terms = [gain * x]
            for n in range(states):
                state[n] = decay[n] * state[n] + x
                terms.append(weight[n] * state[n])
            out_ref[r * SUB : (r + 1) * SUB, :] = added(terms)


def added(terms):
    while len(terms) > 1:
        terms = [
            terms[i] + terms[i + 1] if i + 1 < len(terms) else terms[i]
            for i in range(0, len(terms), 2)
        ]
    return terms[0]


def relay_kernel(share_ref, ends_ref, span_ref, carried_ref):
    devices, rows, _ = ends_ref.shape
    share = share_ref[0]
    forward = share < devices // 2
    start = lax.rem(share, devices // 2) * rows
    span = span_ref[pl.ds(start, rows), :]
    state = jnp.zeros(span.shape, F32)
    for step in range(devices):
        at = jnp.where(forward, step, devices - 1 - step)
        end = ends_ref[at]
        carried_ref[at] = state
        state = span * state + end


def carry_kernel(y_ref, z_ref, rate_ref, weight_ref, carried_ref, out_ref, grad_ref, a_ref, b_ref):
    positions = y_ref.shape[0]
    length = positions // SUB
    states = rate_ref.shape[0]
    rate = rate_ref[...]
    decay_table = jnp.exp(-rate)
    decay = [row_of(decay_table, n) for n in range(states)]
    weight = weight_ref[...]
    block = block_index()
    forward, backward = orders(length)
    after_start = (length * block + 1).astype(F32)
    before_end = (length * (SUB - 1 - block) + 1).astype(F32)
    for side, (ref, scratch, result, order, distance) in enumerate(
        (
            (y_ref, a_ref, out_ref, forward, after_start),
            (z_ref, b_ref, grad_ref, backward, before_end),
        )
    ):
        scaled = weight * carried_ref[side]
        terms = [
            jnp.exp(-row_of(rate, n) * distance) * row_of(scaled, n) for n in range(states)
        ]
        for step, r in enumerate(order):
            if step:
                terms = [decay[n] * terms[n] for n in range(states)]
            total = added(terms + [ref[r * SUB : (r + 1) * SUB, :]])
            scratch[pl.ds(r, SUB, stride=length), :] = total
        result[...] = scratch[...].astype(result.dtype)


def shards(signal, cotangent, decay_rate, residue, skip_gain):
    positions, channels = signal.shape
    states = decay_rate.shape[0]
    columns = channels // LANES
    devices = lax.axis_size("seq")
    grid = (columns,)
    wide = pl.BlockSpec((positions, LANES), lambda c: (0, c))
    state_wide = pl.BlockSpec((states, LANES), lambda c: (0, c))
    one_wide = pl.BlockSpec((1, LANES), lambda c: (0, c))
    stacked = pl.BlockSpec((2, states, LANES), lambda c: (0, c, 0))
    scratch = [pltpu.VMEM((positions, LANES), F32)] * 2
    pair = [jax.ShapeDtypeStruct((positions, channels), F32)] * 2
    elements = positions * channels * states

    ends, span = pl.pallas_call(
        ends_kernel,
        grid=grid,
        in_specs=[wide, wide, state_wide],
        out_specs=[stacked, pl.BlockSpec((states, LANES), lambda c: (c, 0))],
        out_shape=[
            jax.ShapeDtypeStruct((2, columns * states, LANES), F32),
            jax.ShapeDtypeStruct((columns * states, LANES), F32),
        ],
        scratch_shapes=scratch,
        name="ends",
    )(signal, cotangent, decay_rate)

    rows = 2 * columns * states // devices
    sent = ends.reshape(devices, rows, LANES)
    gathered = lax.all_to_all(sent, "seq", 0, 0)

    weight = residue * jnp.sqrt(-jnp.expm1(-2.0 * decay_rate))
    y, z = pl.pallas_call(
        within_kernel,
        grid=grid,
        in_specs=[wide, wide, state_wide, state_wide, one_wide],
        out_specs=[wide, wide],
        out_shape=pair,
        scratch_shapes=scratch,
        cost_estimate=pl.CostEstimate(
            flops=12 * elements, bytes_accessed=12 * positions * channels, transcendentals=0
        ),
        name="within",
    )(signal, cotangent, decay_rate, weight, skip_gain.reshape(1, channels))

    share = lax.axis_index("seq").astype(jnp.int32).reshape(1)
    carried = pl.pallas_call(
        relay_kernel,
        in_specs=[
            pl.BlockSpec(memory_space=pltpu.SMEM),
            pl.BlockSpec(memory_space=pltpu.VMEM),
            pl.BlockSpec(memory_space=pltpu.VMEM),
        ],
        out_specs=pl.BlockSpec(memory_space=pltpu.VMEM),
        out_shape=jax.ShapeDtypeStruct((devices, rows, LANES), F32),
        name="relay",
    )(share, gathered, span)
    returned = lax.all_to_all(carried, "seq", 0, 0).reshape(2, columns * states, LANES)

    return pl.pallas_call(
        carry_kernel,
        grid=grid,
        in_specs=[wide, wide, state_wide, state_wide, stacked],
        out_specs=[wide, wide],
        out_shape=[jax.ShapeDtypeStruct(signal.shape, signal.dtype)] * 2,
        scratch_shapes=scratch,
        name="carry",
    )(y, z, decay_rate, weight, returned)


def solution(mesh):
    in_specs = (P("seq", "chan"), P("seq", "chan"), P(None, "chan"), P(None, "chan"), P("chan"))
    out_specs = (P("seq", "chan"), P("seq", "chan"))
    return jax.shard_map(
        lambda *arrays: tuple(shards(*arrays)),
        mesh=mesh,
        in_specs=in_specs,
        out_specs=out_specs,
        check_vma=False,
    )
```

```python
import functools
import jax
import jax.numpy as jnp
from jax import lax
from jax.experimental import pallas as pl
from jax.experimental.pallas import tpu as pltpu
from jax.sharding import PartitionSpec as P

SUB = 8
LANES = 128
F32 = jnp.float32


def row_of(table, n):
    return jnp.broadcast_to(table[n : n + 1, :], (SUB, LANES))


def block_index():
    return lax.broadcasted_iota(jnp.int32, (SUB, LANES), 0)


def blocked_position(x_ref, r, length):
    return x_ref[pl.ds(r, SUB, stride=length), :]


def block_ends(x_ref, decay, order, length):
    ends = [None] * len(decay)
    for step, r in enumerate(order):
        x = blocked_position(x_ref, r, length)
        for n in range(len(decay)):
            ends[n] = x if step == 0 else decay[n] * ends[n] + x
    return ends


def orders(length):
    return list(range(length)), list(range(length - 1, -1, -1))


def summed_positions(parts):
    at = block_index()
    low = at < 4
    parts = [
        jnp.where(low, parts[i], parts[i + 4])
        + pltpu.roll(jnp.where(low, parts[i + 4], parts[i]), 4, 0)
        for i in range(4)
    ]
    for by in (2, 1):
        low = lax.rem(at, 2 * by) < by
        parts = [
            jnp.where(
                low,
                parts[i] + pltpu.roll(parts[i], SUB - by, 0),
                parts[i + by] + pltpu.roll(parts[i + by], by, 0),
            )
            for i in range(by)
        ]
    return parts[0]


def ends_kernel(
    signal_hbm,
    cotangent_hbm,
    rate_hbm,
    ends_ref,
    signal_ref,
    cotangent_ref,
    rate_ref,
    sems,
    rate_sem,
):
    positions, width = signal_ref.shape
    states = rate_ref.shape[0]
    tiles = positions // SUB

    def part_copies(part):
        lanes = pl.ds(pl.multiple_of(part * 2 * LANES, 2 * LANES), 2 * LANES)
        return [
            pltpu.make_async_copy(hbm.at[:, lanes], ref.at[:, lanes], sems.at[side, part])
            for side, (hbm, ref) in enumerate(
                ((signal_hbm, signal_ref), (cotangent_hbm, cotangent_ref))
            )
        ]

    rate_copy = pltpu.make_async_copy(rate_hbm, rate_ref, rate_sem)
    rate_copy.start()
    for part in range(width // (2 * LANES)):
        for copy in part_copies(part):
            copy.start()
    rate_copy.wait()
    place = block_index()
    after = (SUB - 1 - place).astype(F32)
    before = place.astype(F32)

    def column(c, _):
        lanes = pl.ds(pl.multiple_of(c * LANES, LANES), LANES)
        rate = rate_ref[:, lanes]
        decay_table = jnp.exp(-rate * float(SUB))
        decay = [row_of(decay_table, n) for n in range(states)]
        ends = [None] * states
        starts = [None] * states
        for pair in range(tiles // 2):
            first = pair * 2 * SUB
            x = signal_ref[first : first + 2 * SUB, lanes].astype(F32)
            last = positions - 2 * SUB - first
            g = cotangent_ref[last : last + 2 * SUB, lanes].astype(F32)
            for half in range(2):
                xh = x[half * SUB : (half + 1) * SUB]
                gh = g[(1 - half) * SUB : (2 - half) * SUB]
                for n in range(states):
                    if pair == 0 and half == 0:
                        ends[n], starts[n] = xh, gh
                    else:
                        ends[n] = decay[n] * ends[n] + xh
                        starts[n] = decay[n] * starts[n] + gh
        for side, (sums, distance) in enumerate(((ends, after), (starts, before))):
            for low in range(0, states, SUB):
                parts = [
                    jnp.exp(-row_of(rate, n) * distance) * sums[n]
                    for n in range(low, low + SUB)
                ]
                at = pl.ds(pl.multiple_of(c * states + low, SUB), SUB)
                ends_ref[side, at, :] = summed_positions(parts)
        return 0

    def both_columns(part, _):
        for copy in part_copies(part):
            copy.wait()
        return lax.fori_loop(2 * part, 2 * part + 2, column, 0)

    lax.fori_loop(0, width // (2 * LANES), both_columns, 0)


def entering_states(ends, rate, length, forward):
    block = block_index()
    entering = []
    for n in range(len(ends)):
        total = ends[n]
        reach = 1
        while reach < SUB:
            ratio = jnp.exp(-row_of(rate, n) * float(length * reach))
            total = total + ratio * shifted_blocks(total, reach, block, forward)
            reach *= 2
        entering.append(shifted_blocks(total, 1, block, forward))
    return entering


def shifted_blocks(x, by, block, forward):
    if forward:
        return jnp.where(block >= by, pltpu.roll(x, by, 0), 0.0)
    return jnp.where(block < SUB - by, pltpu.roll(x, SUB - by, 0), 0.0)


def within_kernel(
    is_forward,
    x_hbm,
    rate_hbm,
    weight_hbm,
    gain_hbm,
    *refs,
):
    (
        both_ref,
        span_ref,
        whole_ref,
        x_ref,
        y_ref,
        rate_ref,
        weight_ref,
        gain_ref,
        sems,
        table_sems,
    ) = refs[-10:]
    local_ref = both_ref.at[0 if is_forward else 1]
    positions, width = whole_ref.shape
    length = positions // SUB
    states = rate_ref.shape[0]
    order = orders(length)[0 if is_forward else 1]
    place = block_index()
    distance = (place + 1 if is_forward else SUB - place).astype(F32)

    def part_copy(part):
        lanes = pl.ds(pl.multiple_of(part * 2 * LANES, 2 * LANES), 2 * LANES)
        return pltpu.make_async_copy(x_hbm.at[:, lanes], whole_ref.at[:, lanes], sems.at[part])

    table_copies = [
        pltpu.make_async_copy(hbm, ref, table_sems.at[i])
        for i, (hbm, ref) in enumerate(
            ((rate_hbm, rate_ref), (weight_hbm, weight_ref), (gain_hbm, gain_ref))
        )
    ]
    for copy in table_copies:
        copy.start()
    for part in range(width // (2 * LANES)):
        part_copy(part).start()
    for copy in table_copies:
        copy.wait()

    def column(c, _):
        lanes = pl.ds(pl.multiple_of(c * LANES, LANES), LANES)
        x_ref[...] = whole_ref[:, lanes].astype(F32)
        rate = rate_ref[:, lanes]
        rows = pl.ds(pl.multiple_of(c * states, states), states)
        span_ref[rows, :] = jnp.exp(-rate * float(positions))
        decay_table = jnp.exp(-rate)
        decay = [row_of(decay_table, n) for n in range(states)]
        weight_table = weight_ref[:, lanes]
        weight = [row_of(weight_table, n) for n in range(states)]
        gain = jnp.broadcast_to(gain_ref[:, lanes], (SUB, LANES))
        for n in range(states):
            reach = jnp.exp(-row_of(rate, n) * distance)
            local_ref[pl.ds(positions + n * SUB, SUB), lanes] = weight[n] * reach
        ends = block_ends(x_ref, decay, order, length)
        state = entering_states(ends, rate, length, is_forward)
        for r in order:
            x = blocked_position(x_ref, r, length)
            terms = [gain * x]
            for n in range(states):
                state[n] = decay[n] * state[n] + x
                terms.append(weight[n] * state[n])
            y_ref[pl.ds(r, SUB, stride=length), :] = added(terms)
        local_ref[pl.ds(0, positions), lanes] = y_ref[...]
        return 0

    def both_columns(part, _):
        part_copy(part).wait()
        return lax.fori_loop(2 * part, 2 * part + 2, column, 0)

    lax.fori_loop(0, width // (2 * LANES), both_columns, 0)


def added(terms):
    while len(terms) > 1:
        terms = [
            terms[i] + terms[i + 1] if i + 1 < len(terms) else terms[i]
            for i in range(0, len(terms), 2)
        ]
    return terms[0]


def relay_kernel(share_ref, ends_ref, span_ref, carried_ref):
    devices, rows, _ = ends_ref.shape
    share = share_ref[0]
    forward = share < devices // 2
    span = span_ref[pl.ds(lax.rem(share, devices // 2) * rows, rows), :]
    state = jnp.zeros(span.shape, F32)
    for step in range(devices):
        at = jnp.where(forward, step, devices - 1 - step)
        end = ends_ref[at]
        carried_ref[at] = state
        state = span * state + end


def carry_kernel(
    both_ref, rate_ref, carried_ref, out_hbm, grad_hbm, out_ref, grad_ref, sems
):
    positions, width = out_ref.shape
    states = rate_ref.shape[0]
    tiles = positions // SUB

    def part_copies(part):
        lanes = pl.ds(pl.multiple_of(part * 2 * LANES, 2 * LANES), 2 * LANES)
        return [
            pltpu.make_async_copy(ref.at[:, lanes], hbm.at[:, lanes], sems.at[side, part])
            for side, (hbm, ref) in enumerate(((out_hbm, out_ref), (grad_hbm, grad_ref)))
        ]

    def column(c, _):
        lanes = pl.ds(pl.multiple_of(c * LANES, LANES), LANES)
        decay_table = jnp.exp(-rate_ref[:, lanes] * float(SUB))
        decay = [row_of(decay_table, n) for n in range(states)]
        rows = pl.ds(pl.multiple_of(c * states, states), states)
        for side, result in enumerate((out_ref, grad_ref)):
            local_ref = both_ref.at[side]
            carried = carried_ref[side, rows, :]
            terms = [
                local_ref[pl.ds(positions + n * SUB, SUB), lanes] * row_of(carried, n)
                for n in range(states)
            ]
            for pair in range(tiles // 2):
                halves = []
                first = pair * 2 * SUB if side == 0 else positions - (pair + 1) * 2 * SUB
                for half in range(2):
                    if pair or half:
                        terms = [decay[n] * terms[n] for n in range(states)]
                    start = first + (half if side == 0 else 1 - half) * SUB
                    local = local_ref[pl.ds(start, SUB), lanes]
                    halves.append(added(terms) + local)
                if side:
                    halves.reverse()
                both = jnp.concatenate(halves, axis=0)
                result[first : first + 2 * SUB, lanes] = both.astype(result.dtype)
        return 0

    def both_columns(part, _):
        lax.fori_loop(2 * part, 2 * part + 2, column, 0)
        for copy in part_copies(part):
            copy.start()
        return 0

    lax.fori_loop(0, width // (2 * LANES), both_columns, 0)
    for part in range(width // (2 * LANES)):
        for copy in part_copies(part):
            copy.wait()


def vmem(mib):
    return pltpu.CompilerParams(vmem_limit_bytes=mib << 20)


def shards(signal, cotangent, decay_rate, residue, skip_gain):
    positions, channels = signal.shape
    states = decay_rate.shape[0]
    columns = channels // LANES
    devices = lax.axis_size("seq")
    anywhere = pl.BlockSpec(memory_space=pl.ANY)
    in_hbm = pl.BlockSpec(memory_space=pltpu.HBM)
    in_vmem = pl.BlockSpec(memory_space=pltpu.VMEM)
    elements = positions * channels * states
    whole = pltpu.VMEM((positions, channels), signal.dtype)
    column = pltpu.VMEM((positions, LANES), F32)
    table = pltpu.VMEM(decay_rate.shape, F32)
    copy_sems = pltpu.SemaphoreType.DMA((2, columns // 2))

    ends = pl.pallas_call(
        ends_kernel,
        in_specs=[in_hbm] * 3,
        out_specs=in_vmem,
        out_shape=jax.ShapeDtypeStruct((2, columns * states, LANES), F32),
        scratch_shapes=[
            whole,
            whole,
            table,
            copy_sems,
            pltpu.SemaphoreType.DMA,
        ],
        compiler_params=vmem(56),
        name="ends",
    )(signal, cotangent, decay_rate)

    rows = 2 * columns * states // devices
    sent = ends.reshape(devices, rows, LANES)
    gathered = lax.all_to_all(sent, "seq", 0, 0)

    weight = residue * jnp.sqrt(-jnp.expm1(-2.0 * decay_rate))
    gain = skip_gain.reshape(1, channels)
    depth = positions + states * SUB

    def within(is_forward, x, *other):
        return pl.pallas_call(
            functools.partial(within_kernel, is_forward),
            in_specs=[in_hbm] * 4 + [in_vmem] * len(other),
            out_specs=[in_vmem] * 2,
            out_shape=[
                jax.ShapeDtypeStruct((2, depth, channels), F32),
                jax.ShapeDtypeStruct((columns * states, LANES), F32),
            ],
            input_output_aliases={4: 0} if other else {},
            scratch_shapes=[
                whole,
                column,
                column,
                table,
                table,
                pltpu.VMEM((1, channels), F32),
                pltpu.SemaphoreType.DMA((columns // 2,)),
                pltpu.SemaphoreType.DMA((3,)),
            ],
            cost_estimate=pl.CostEstimate(
                flops=6 * elements, bytes_accessed=6 * positions * channels, transcendentals=0
            ),
            compiler_params=vmem(8),
            name="within_forward" if is_forward else "within_backward",
        )(x, decay_rate, weight, gain, *other)

    half, span = within(True, signal)
    both, _ = within(False, cotangent, half)
    share = lax.axis_index("seq").astype(jnp.int32).reshape(1)
    carried = pl.pallas_call(
        relay_kernel,
        in_specs=[pl.BlockSpec(memory_space=pltpu.SMEM), in_vmem, in_vmem],
        out_specs=in_vmem,
        out_shape=jax.ShapeDtypeStruct((devices, rows, LANES), F32),
        compiler_params=vmem(4),
        name="relay",
    )(share, gathered, span)
    returned = lax.all_to_all(carried, "seq", 0, 0).reshape(2, columns * states, LANES)

    return pl.pallas_call(
        carry_kernel,
        in_specs=[in_vmem] * 3,
        out_specs=[in_hbm] * 2,
        out_shape=[jax.ShapeDtypeStruct(signal.shape, signal.dtype)] * 2,
        scratch_shapes=[whole, whole, copy_sems],
        compiler_params=vmem(8),
        name="carry",
    )(both, decay_rate, returned)


def solution(mesh):
    in_specs = (P("seq", "chan"), P("seq", "chan"), P(None, "chan"), P(None, "chan"), P("chan"))
    out_specs = (P("seq", "chan"), P("seq", "chan"))
    return jax.shard_map(
        lambda *arrays: tuple(shards(*arrays)),
        mesh=mesh,
        in_specs=in_specs,
        out_specs=out_specs,
        check_vma=False,
    )
```

```python
import functools
import jax
import jax.numpy as jnp
from jax import lax
from jax.experimental import pallas as pl
from jax.experimental.pallas import tpu as pltpu
from jax.sharding import PartitionSpec as P

SUB = 8
LANES = 128
F32 = jnp.float32


def row_of(table, n):
    return jnp.broadcast_to(table[n : n + 1, :], (SUB, LANES))


def block_index():
    return lax.broadcasted_iota(jnp.int32, (SUB, LANES), 0)


def blocked_position(x_ref, r, length):
    return x_ref[pl.ds(r, SUB, stride=length), :]


def block_ends(x_ref, decay, order, length):
    ends = [None] * len(decay)
    for step, r in enumerate(order):
        x = blocked_position(x_ref, r, length)
        for n in range(len(decay)):
            ends[n] = x if step == 0 else decay[n] * ends[n] + x
    return ends


def orders(length):
    return list(range(length)), list(range(length - 1, -1, -1))


def summed_positions(parts):
    at = block_index()
    low = at < 4
    parts = [
        jnp.where(low, parts[i], parts[i + 4])
        + pltpu.roll(jnp.where(low, parts[i + 4], parts[i]), 4, 0)
        for i in range(4)
    ]
    for by in (2, 1):
        low = lax.rem(at, 2 * by) < by
        parts = [
            jnp.where(
                low,
                parts[i] + pltpu.roll(parts[i], SUB - by, 0),
                parts[i + by] + pltpu.roll(parts[i + by], by, 0),
            )
            for i in range(by)
        ]
    return parts[0]


def ends_kernel(
    signal_hbm,
    cotangent_hbm,
    rate_hbm,
    ends_ref,
    signal_ref,
    cotangent_ref,
    rate_ref,
    sems,
    rate_sem,
):
    positions, width = signal_ref.shape
    states = rate_ref.shape[0]
    tiles = positions // SUB

    def part_copies(part):
        lanes = pl.ds(pl.multiple_of(part * 2 * LANES, 2 * LANES), 2 * LANES)
        return [
            pltpu.make_async_copy(hbm.at[:, lanes], ref.at[:, lanes], sems.at[side, part])
            for side, (hbm, ref) in enumerate(
                ((signal_hbm, signal_ref), (cotangent_hbm, cotangent_ref))
            )
        ]

    rate_copy = pltpu.make_async_copy(rate_hbm, rate_ref, rate_sem)
    rate_copy.start()
    for part in range(width // (2 * LANES)):
        for copy in part_copies(part):
            copy.start()
    rate_copy.wait()
    place = block_index()
    after = (SUB - 1 - place).astype(F32)
    before = place.astype(F32)

    def column(c, _):
        lanes = pl.ds(pl.multiple_of(c * LANES, LANES), LANES)
        rate = rate_ref[:, lanes]
        decay_table = jnp.exp(-rate * float(SUB))
        decay = [row_of(decay_table, n) for n in range(states)]
        ends = [None] * states
        starts = [None] * states
        for pair in range(tiles // 2):
            first = pair * 2 * SUB
            x = signal_ref[first : first + 2 * SUB, lanes].astype(F32)
            last = positions - 2 * SUB - first
            g = cotangent_ref[last : last + 2 * SUB, lanes].astype(F32)
            for half in range(2):
                xh = x[half * SUB : (half + 1) * SUB]
                gh = g[(1 - half) * SUB : (2 - half) * SUB]
                for n in range(states):
                    if pair == 0 and half == 0:
                        ends[n], starts[n] = xh, gh
                    else:
                        ends[n] = decay[n] * ends[n] + xh
                        starts[n] = decay[n] * starts[n] + gh
        for side, (sums, distance) in enumerate(((ends, after), (starts, before))):
            for low in range(0, states, SUB):
                parts = [
                    jnp.exp(-row_of(rate, n) * distance) * sums[n]
                    for n in range(low, low + SUB)
                ]
                at = pl.ds(pl.multiple_of(c * states + low, SUB), SUB)
                ends_ref[side, at, :] = summed_positions(parts)
        return 0

    def both_columns(part, _):
        for copy in part_copies(part):
            copy.wait()
        return lax.fori_loop(2 * part, 2 * part + 2, column, 0)

    lax.fori_loop(0, width // (2 * LANES), both_columns, 0)


def entering_states(ends, rate, length, forward):
    block = block_index()
    entering = []
    for n in range(len(ends)):
        total = ends[n]
        reach = 1
        while reach < SUB:
            ratio = jnp.exp(-row_of(rate, n) * float(length * reach))
            total = total + ratio * shifted_blocks(total, reach, block, forward)
            reach *= 2
        entering.append(shifted_blocks(total, 1, block, forward))
    return entering


def shifted_blocks(x, by, block, forward):
    if forward:
        return jnp.where(block >= by, pltpu.roll(x, by, 0), 0.0)
    return jnp.where(block < SUB - by, pltpu.roll(x, SUB - by, 0), 0.0)


def within_kernel(
    is_forward,
    x_hbm,
    rate_hbm,
    weight_hbm,
    gain_hbm,
    *refs,
):
    (
        both_ref,
        whole_ref,
        x_ref,
        y_ref,
        rate_ref,
        weight_ref,
        gain_ref,
        sems,
        table_sems,
    ) = refs[-9:]
    local_ref = both_ref.at[0 if is_forward else 1]
    positions, width = whole_ref.shape
    length = positions // SUB
    states = rate_ref.shape[0]
    order = orders(length)[0 if is_forward else 1]
    place = block_index()
    distance = (place + 1 if is_forward else SUB - place).astype(F32)

    def part_copy(part):
        lanes = pl.ds(pl.multiple_of(part * 2 * LANES, 2 * LANES), 2 * LANES)
        return pltpu.make_async_copy(x_hbm.at[:, lanes], whole_ref.at[:, lanes], sems.at[part])

    table_copies = [
        pltpu.make_async_copy(hbm, ref, table_sems.at[i])
        for i, (hbm, ref) in enumerate(
            ((rate_hbm, rate_ref), (weight_hbm, weight_ref), (gain_hbm, gain_ref))
        )
    ]
    for copy in table_copies:
        copy.start()
    for part in range(width // (2 * LANES)):
        part_copy(part).start()
    for copy in table_copies:
        copy.wait()

    def column(c, _):
        lanes = pl.ds(pl.multiple_of(c * LANES, LANES), LANES)
        x_ref[...] = whole_ref[:, lanes].astype(F32)
        rate = rate_ref[:, lanes]
        decay_table = jnp.exp(-rate)
        decay = [row_of(decay_table, n) for n in range(states)]
        weight_table = weight_ref[:, lanes]
        weight = [row_of(weight_table, n) for n in range(states)]
        gain = jnp.broadcast_to(gain_ref[:, lanes], (SUB, LANES))
        for n in range(states):
            reach = jnp.exp(-row_of(rate, n) * distance)
            local_ref[pl.ds(positions + n * SUB, SUB), lanes] = weight[n] * reach
        ends = block_ends(x_ref, decay, order, length)
        state = entering_states(ends, rate, length, is_forward)
        for r in order:
            x = blocked_position(x_ref, r, length)
            terms = [gain * x]
            for n in range(states):
                state[n] = decay[n] * state[n] + x
                terms.append(weight[n] * state[n])
            y_ref[pl.ds(r, SUB, stride=length), :] = added(terms)
        local_ref[pl.ds(0, positions), lanes] = y_ref[...]
        return 0

    def both_columns(part, _):
        part_copy(part).wait()
        return lax.fori_loop(2 * part, 2 * part + 2, column, 0)

    lax.fori_loop(0, width // (2 * LANES), both_columns, 0)


def added(terms):
    while len(terms) > 1:
        terms = [
            terms[i] + terms[i + 1] if i + 1 < len(terms) else terms[i]
            for i in range(0, len(terms), 2)
        ]
    return terms[0]


def relay_kernel(share_ref, ends_ref, span_ref, carried_ref):
    devices, rows, _ = ends_ref.shape
    share = share_ref[0]
    forward = share < devices // 2
    span = span_ref[pl.ds(lax.rem(share, devices // 2) * rows, rows), :]
    state = jnp.zeros(span.shape, F32)
    for step in range(devices):
        at = jnp.where(forward, step, devices - 1 - step)
        end = ends_ref[at]
        carried_ref[at] = state
        state = span * state + end


def carry_kernel(
    both_ref, rate_ref, carried_ref, out_hbm, grad_hbm, out_ref, grad_ref, sems
):
    positions, width = out_ref.shape
    states = rate_ref.shape[0]
    tiles = positions // SUB

    def part_copies(part):
        lanes = pl.ds(pl.multiple_of(part * 2 * LANES, 2 * LANES), 2 * LANES)
        return [
            pltpu.make_async_copy(ref.at[:, lanes], hbm.at[:, lanes], sems.at[side, part])
            for side, (hbm, ref) in enumerate(((out_hbm, out_ref), (grad_hbm, grad_ref)))
        ]

    def column(c, _):
        lanes = pl.ds(pl.multiple_of(c * LANES, LANES), LANES)
        decay_table = jnp.exp(-rate_ref[:, lanes] * float(SUB))
        decay = [row_of(decay_table, n) for n in range(states)]
        rows = pl.ds(pl.multiple_of(c * states, states), states)
        for side, result in enumerate((out_ref, grad_ref)):
            local_ref = both_ref.at[side]
            carried = carried_ref[side, rows, :]
            terms = [
                local_ref[pl.ds(positions + n * SUB, SUB), lanes] * row_of(carried, n)
                for n in range(states)
            ]
            for pair in range(tiles // 2):
                halves = []
                first = pair * 2 * SUB if side == 0 else positions - (pair + 1) * 2 * SUB
                for half in range(2):
                    if pair or half:
                        terms = [decay[n] * terms[n] for n in range(states)]
                    start = first + (half if side == 0 else 1 - half) * SUB
                    local = local_ref[pl.ds(start, SUB), lanes]
                    halves.append(added(terms) + local)
                if side:
                    halves.reverse()
                both = jnp.concatenate(halves, axis=0)
                result[first : first + 2 * SUB, lanes] = both.astype(result.dtype)
        return 0

    def both_columns(part, _):
        lax.fori_loop(2 * part, 2 * part + 2, column, 0)
        for copy in part_copies(part):
            copy.start()
        return 0

    lax.fori_loop(0, width // (2 * LANES), both_columns, 0)
    for part in range(width // (2 * LANES)):
        for copy in part_copies(part):
            copy.wait()


def vmem(mib):
    return pltpu.CompilerParams(vmem_limit_bytes=mib << 20)


def shards(signal, cotangent, decay_rate, residue, skip_gain):
    positions, channels = signal.shape
    states = decay_rate.shape[0]
    columns = channels // LANES
    devices = lax.axis_size("seq")
    anywhere = pl.BlockSpec(memory_space=pl.ANY)
    in_hbm = pl.BlockSpec(memory_space=pltpu.HBM)
    in_vmem = pl.BlockSpec(memory_space=pltpu.VMEM)
    elements = positions * channels * states
    whole = pltpu.VMEM((positions, channels), signal.dtype)
    column = pltpu.VMEM((positions, LANES), F32)
    table = pltpu.VMEM(decay_rate.shape, F32)
    copy_sems = pltpu.SemaphoreType.DMA((2, columns // 2))

    ends = pl.pallas_call(
        ends_kernel,
        in_specs=[in_hbm] * 3,
        out_specs=in_vmem,
        out_shape=jax.ShapeDtypeStruct((2, columns * states, LANES), F32),
        scratch_shapes=[
            whole,
            whole,
            table,
            copy_sems,
            pltpu.SemaphoreType.DMA,
        ],
        compiler_params=vmem(56),
        name="ends",
    )(signal, cotangent, decay_rate)

    rows = 2 * columns * states // devices
    sent = ends.reshape(devices, rows, LANES)
    gathered = lax.all_to_all(sent, "seq", 0, 0)

    weight = residue * jnp.sqrt(-jnp.expm1(-2.0 * decay_rate))
    gain = skip_gain.reshape(1, channels)
    depth = positions + states * SUB

    def within(is_forward, x, *other):
        return pl.pallas_call(
            functools.partial(within_kernel, is_forward),
            in_specs=[in_hbm] * 4 + [in_vmem] * len(other),
            out_specs=in_vmem,
            out_shape=jax.ShapeDtypeStruct((2, depth, channels), F32),
            input_output_aliases={4: 0} if other else {},
            scratch_shapes=[
                whole,
                column,
                column,
                table,
                table,
                pltpu.VMEM((1, channels), F32),
                pltpu.SemaphoreType.DMA((columns // 2,)),
                pltpu.SemaphoreType.DMA((3,)),
            ],
            cost_estimate=pl.CostEstimate(
                flops=6 * elements, bytes_accessed=6 * positions * channels, transcendentals=0
            ),
            compiler_params=vmem(8),
            name="within_forward" if is_forward else "within_backward",
        )(x, decay_rate, weight, gain, *other)

    rate_then, _ = lax.optimization_barrier((decay_rate, ends))
    span = jnp.exp(-float(positions) * rate_then).reshape(states, columns, LANES)
    span = span.swapaxes(0, 1).reshape(columns * states, LANES)

    share = lax.axis_index("seq").astype(jnp.int32).reshape(1)
    carried = pl.pallas_call(
        relay_kernel,
        in_specs=[pl.BlockSpec(memory_space=pltpu.SMEM), in_vmem, in_vmem],
        out_specs=in_vmem,
        out_shape=jax.ShapeDtypeStruct((devices, rows, LANES), F32),
        compiler_params=vmem(4),
        name="relay",
    )(share, gathered, span)
    signal, cotangent, _ = lax.optimization_barrier((signal, cotangent, carried))
    both = within(False, cotangent, within(True, signal))
    returned = lax.all_to_all(carried, "seq", 0, 0).reshape(2, columns * states, LANES)

    return pl.pallas_call(
        carry_kernel,
        in_specs=[in_vmem] * 3,
        out_specs=[in_hbm] * 2,
        out_shape=[jax.ShapeDtypeStruct(signal.shape, signal.dtype)] * 2,
        scratch_shapes=[whole, whole, copy_sems],
        compiler_params=vmem(8),
        name="carry",
    )(both, decay_rate, returned)


def solution(mesh):
    in_specs = (P("seq", "chan"), P("seq", "chan"), P(None, "chan"), P(None, "chan"), P("chan"))
    out_specs = (P("seq", "chan"), P("seq", "chan"))
    return jax.shard_map(
        lambda *arrays: tuple(shards(*arrays)),
        mesh=mesh,
        in_specs=in_specs,
        out_specs=out_specs,
        check_vma=False,
    )
```

```python
import functools
import jax
import jax.numpy as jnp
from jax import lax
from jax.experimental import pallas as pl
from jax.experimental.pallas import tpu as pltpu
from jax.sharding import PartitionSpec as P

SUB = 8
LANES = 128
F32 = jnp.float32
ROOT, ROOT_OF = 41, 64


def row_of(table, n):
    return jnp.broadcast_to(table[n : n + 1, :], (SUB, LANES))


def block_index():
    return lax.broadcasted_iota(jnp.int32, (SUB, LANES), 0)


def blocked_position(x_ref, r, length):
    return x_ref[pl.ds(r, SUB, stride=length), :]


def block_ends(x_ref, decay, order, length):
    ends = [None] * len(decay)
    for step, r in enumerate(order):
        x = blocked_position(x_ref, r, length)
        for n in range(len(decay)):
            ends[n] = x if step == 0 else decay[n] * ends[n] + x
    return ends


def orders(length):
    return list(range(length)), list(range(length - 1, -1, -1))


def summed_positions(parts):
    at = block_index()
    low = at < 4
    parts = [
        jnp.where(low, parts[i], parts[i + 4])
        + pltpu.roll(jnp.where(low, parts[i + 4], parts[i]), 4, 0)
        for i in range(4)
    ]
    for by in (2, 1):
        low = lax.rem(at, 2 * by) < by
        parts = [
            jnp.where(
                low,
                parts[i] + pltpu.roll(parts[i], SUB - by, 0),
                parts[i + by] + pltpu.roll(parts[i + by], by, 0),
            )
            for i in range(by)
        ]
    return parts[0]


def ends_kernel(
    signal_hbm,
    cotangent_hbm,
    rate_hbm,
    ends_ref,
    signal_ref,
    cotangent_ref,
    rate_ref,
    sems,
    rate_sem,
):
    positions, width = signal_ref.shape
    states = rate_ref.shape[0]
    tiles = positions // SUB

    def part_copies(part):
        lanes = pl.ds(pl.multiple_of(part * 2 * LANES, 2 * LANES), 2 * LANES)
        return [
            pltpu.make_async_copy(hbm.at[:, lanes], ref.at[:, lanes], sems.at[side, part])
            for side, (hbm, ref) in enumerate(
                ((signal_hbm, signal_ref), (cotangent_hbm, cotangent_ref))
            )
        ]

    rate_copy = pltpu.make_async_copy(rate_hbm, rate_ref, rate_sem)
    rate_copy.start()
    for part in range(width // (2 * LANES)):
        for copy in part_copies(part):
            copy.start()
    rate_copy.wait()
    place = block_index()
    after = (SUB - 1 - place).astype(F32)
    before = place.astype(F32)

    def column(c, _):
        lanes = pl.ds(pl.multiple_of(c * LANES, LANES), LANES)
        rate = rate_ref[:, lanes]
        decay_table = jnp.exp(-rate * float(SUB))
        decay = [row_of(decay_table, n) for n in range(states)]
        ends = [None] * states
        starts = [None] * states
        for pair in range(tiles // 2):
            first = pair * 2 * SUB
            x = signal_ref[first : first + 2 * SUB, lanes].astype(F32)
            last = positions - 2 * SUB - first
            g = cotangent_ref[last : last + 2 * SUB, lanes].astype(F32)
            for half in range(2):
                xh = x[half * SUB : (half + 1) * SUB]
                gh = g[(1 - half) * SUB : (2 - half) * SUB]
                for n in range(states):
                    if pair == 0 and half == 0:
                        ends[n], starts[n] = xh, gh
                    else:
                        ends[n] = decay[n] * ends[n] + xh
                        starts[n] = decay[n] * starts[n] + gh
        for side, (sums, distance) in enumerate(((ends, after), (starts, before))):
            for low in range(0, states, SUB):
                parts = [
                    jnp.exp(-row_of(rate, n) * distance) * sums[n]
                    for n in range(low, low + SUB)
                ]
                at = pl.ds(pl.multiple_of(c * states + low, SUB), SUB)
                ends_ref[side, at, :] = summed_positions(parts)
        return 0

    def both_columns(part, _):
        for copy in part_copies(part):
            copy.wait()
        return lax.fori_loop(2 * part, 2 * part + 2, column, 0)

    lax.fori_loop(0, width // (2 * LANES), both_columns, 0)


def entering_states(ends, rate, length, forward):
    block = block_index()
    entering = []
    for n in range(len(ends)):
        total = ends[n]
        reach = 1
        while reach < SUB:
            ratio = jnp.exp(-row_of(rate, n) * float(length * reach))
            total = total + ratio * shifted_blocks(total, reach, block, forward)
            reach *= 2
        entering.append(shifted_blocks(total, 1, block, forward))
    return entering


def shifted_blocks(x, by, block, forward):
    if forward:
        return jnp.where(block >= by, pltpu.roll(x, by, 0), 0.0)
    return jnp.where(block < SUB - by, pltpu.roll(x, SUB - by, 0), 0.0)


def within_kernel(
    is_forward,
    x_hbm,
    rate_hbm,
    weight_hbm,
    gain_hbm,
    *refs,
):
    (
        both_ref,
        whole_ref,
        x_ref,
        y_ref,
        rate_ref,
        weight_ref,
        gain_ref,
        sems,
        table_sems,
    ) = refs[-9:]
    local_ref = both_ref.at[0 if is_forward else 1]
    positions, width = whole_ref.shape
    length = positions // SUB
    states = rate_ref.shape[0]
    order = orders(length)[0 if is_forward else 1]
    place = block_index()
    distance = (place + 1 if is_forward else SUB - place).astype(F32)

    def part_copy(part):
        lanes = pl.ds(pl.multiple_of(part * 2 * LANES, 2 * LANES), 2 * LANES)
        return pltpu.make_async_copy(x_hbm.at[:, lanes], whole_ref.at[:, lanes], sems.at[part])

    table_copies = [
        pltpu.make_async_copy(hbm, ref, table_sems.at[i])
        for i, (hbm, ref) in enumerate(
            ((rate_hbm, rate_ref), (weight_hbm, weight_ref), (gain_hbm, gain_ref))
        )
    ]
    for copy in table_copies:
        copy.start()
    for part in range(width // (2 * LANES)):
        part_copy(part).start()
    for copy in table_copies:
        copy.wait()

    def column(c, _):
        lanes = pl.ds(pl.multiple_of(c * LANES, LANES), LANES)
        x_ref[...] = whole_ref[:, lanes].astype(F32)
        rate = rate_ref[:, lanes]
        decay_table = jnp.exp(-rate)
        decay = [row_of(decay_table, n) for n in range(states)]
        weight_table = weight_ref[:, lanes]
        weight = [row_of(weight_table, n) for n in range(states)]
        gain = jnp.broadcast_to(gain_ref[:, lanes], (SUB, LANES))
        for n in range(states):
            reach = jnp.exp(-row_of(rate, n) * distance)
            local_ref[pl.ds(positions + n * SUB, SUB), lanes] = weight[n] * reach
        ends = block_ends(x_ref, decay, order, length)
        state = entering_states(ends, rate, length, is_forward)
        for r in order:
            x = blocked_position(x_ref, r, length)
            terms = [gain * x]
            for n in range(states):
                state[n] = decay[n] * state[n] + x
                terms.append(weight[n] * state[n])
            y_ref[pl.ds(r, SUB, stride=length), :] = added(terms)
        local_ref[pl.ds(0, positions), lanes] = y_ref[...]
        return 0

    def both_columns(part, _):
        part_copy(part).wait()
        return lax.fori_loop(2 * part, 2 * part + 2, column, 0)

    lax.fori_loop(0, width // (2 * LANES), both_columns, 0)


def added(terms):
    while len(terms) > 1:
        terms = [
            terms[i] + terms[i + 1] if i + 1 < len(terms) else terms[i]
            for i in range(0, len(terms), 2)
        ]
    return terms[0]


def relay_kernel(first, share_ref, ends_ref, span_ref, carried_ref):
    devices, rows, _ = ends_ref.shape
    share = share_ref[0]
    forward = share < devices // 2
    span = span_ref[pl.ds(lax.rem(share, devices // 2) * rows, rows), :]
    state = jnp.zeros(span.shape, F32)
    for step in range(devices):
        ahead, behind = (step - first) % devices, (devices - 1 - step - first) % devices
        at = jnp.where(forward, ahead, behind)
        end = ends_ref[at]
        carried_ref[at] = state
        state = span * state + end


def carry_kernel(
    both_ref, rate_ref, carried_ref, out_hbm, grad_hbm, out_ref, grad_ref, sems
):
    positions, width = out_ref.shape
    states = rate_ref.shape[0]
    tiles = positions // SUB

    def part_copies(part):
        lanes = pl.ds(pl.multiple_of(part * 2 * LANES, 2 * LANES), 2 * LANES)
        return [
            pltpu.make_async_copy(ref.at[:, lanes], hbm.at[:, lanes], sems.at[side, part])
            for side, (hbm, ref) in enumerate(((out_hbm, out_ref), (grad_hbm, grad_ref)))
        ]

    def column(c, _):
        lanes = pl.ds(pl.multiple_of(c * LANES, LANES), LANES)
        decay_table = jnp.exp(-rate_ref[:, lanes] * float(SUB))
        decay = [row_of(decay_table, n) for n in range(states)]
        rows = pl.ds(pl.multiple_of(c * states, states), states)
        for side, result in enumerate((out_ref, grad_ref)):
            local_ref = both_ref.at[side]
            carried = carried_ref[side, rows, :]
            terms = [
                local_ref[pl.ds(positions + n * SUB, SUB), lanes] * row_of(carried, n)
                for n in range(states)
            ]
            for pair in range(tiles // 2):
                halves = []
                first = pair * 2 * SUB if side == 0 else positions - (pair + 1) * 2 * SUB
                for half in range(2):
                    if pair or half:
                        terms = [decay[n] * terms[n] for n in range(states)]
                    start = first + (half if side == 0 else 1 - half) * SUB
                    local = local_ref[pl.ds(start, SUB), lanes]
                    halves.append(added(terms) + local)
                if side:
                    halves.reverse()
                both = jnp.concatenate(halves, axis=0)
                result[first : first + 2 * SUB, lanes] = both.astype(result.dtype)
        return 0

    def both_columns(part, _):
        lax.fori_loop(2 * part, 2 * part + 2, column, 0)
        for copy in part_copies(part):
            copy.start()
        return 0

    lax.fori_loop(0, width // (2 * LANES), both_columns, 0)
    for part in range(width // (2 * LANES)):
        for copy in part_copies(part):
            copy.wait()


def vmem(mib):
    return pltpu.CompilerParams(vmem_limit_bytes=mib << 20)


def shards(signal, cotangent, decay_rate, residue, skip_gain):
    positions, channels = signal.shape
    states = decay_rate.shape[0]
    columns = channels // LANES
    devices = lax.axis_size("seq")
    anywhere = pl.BlockSpec(memory_space=pl.ANY)
    in_hbm = pl.BlockSpec(memory_space=pltpu.HBM)
    in_vmem = pl.BlockSpec(memory_space=pltpu.VMEM)
    elements = positions * channels * states
    whole = pltpu.VMEM((positions, channels), signal.dtype)
    column = pltpu.VMEM((positions, LANES), F32)
    table = pltpu.VMEM(decay_rate.shape, F32)
    copy_sems = pltpu.SemaphoreType.DMA((2, columns // 2))

    ends = pl.pallas_call(
        ends_kernel,
        in_specs=[in_hbm] * 3,
        out_specs=in_vmem,
        out_shape=jax.ShapeDtypeStruct((2, columns * states, LANES), F32),
        scratch_shapes=[
            whole,
            whole,
            table,
            copy_sems,
            pltpu.SemaphoreType.DMA,
        ],
        compiler_params=vmem(56),
        name="ends",
    )(signal, cotangent, decay_rate)

    rows = 2 * columns * states // devices
    sent = ends.reshape(devices, rows, LANES)
    first = ROOT * devices // ROOT_OF
    group = [[(first + i) % devices for i in range(devices)]]
    exchanged = functools.partial(
        lax.all_to_all,
        axis_name="seq",
        split_axis=0,
        concat_axis=0,
        axis_index_groups=group,
    )
    gathered = exchanged(sent)

    weight = residue * jnp.sqrt(-jnp.expm1(-2.0 * decay_rate))
    gain = skip_gain.reshape(1, channels)
    depth = positions + states * SUB

    def within(is_forward, x, *other):
        return pl.pallas_call(
            functools.partial(within_kernel, is_forward),
            in_specs=[in_hbm] * 4 + [in_vmem] * len(other),
            out_specs=in_vmem,
            out_shape=jax.ShapeDtypeStruct((2, depth, channels), F32),
            input_output_aliases={4: 0} if other else {},
            scratch_shapes=[
                whole,
                column,
                column,
                table,
                table,
                pltpu.VMEM((1, channels), F32),
                pltpu.SemaphoreType.DMA((columns // 2,)),
                pltpu.SemaphoreType.DMA((3,)),
            ],
            cost_estimate=pl.CostEstimate(
                flops=6 * elements, bytes_accessed=6 * positions * channels, transcendentals=0
            ),
            compiler_params=vmem(8),
            name="within_forward" if is_forward else "within_backward",
        )(x, decay_rate, weight, gain, *other)

    rate_then, _ = lax.optimization_barrier((decay_rate, ends))
    span = jnp.exp(-float(positions) * rate_then).reshape(states, columns, LANES)
    span = span.swapaxes(0, 1).reshape(columns * states, LANES)

    share = lax.rem(lax.axis_index("seq") + (devices - first), devices)
    share = share.astype(jnp.int32).reshape(1)
    carried = pl.pallas_call(
        functools.partial(relay_kernel, first),
        in_specs=[pl.BlockSpec(memory_space=pltpu.SMEM), in_vmem, in_vmem],
        out_specs=in_vmem,
        out_shape=jax.ShapeDtypeStruct((devices, rows, LANES), F32),
        compiler_params=vmem(4),
        name="relay",
    )(share, gathered, span)
    signal, cotangent, _ = lax.optimization_barrier((signal, cotangent, carried))
    both = within(False, cotangent, within(True, signal))
    returned = exchanged(carried).reshape(2, columns * states, LANES)

    return pl.pallas_call(
        carry_kernel,
        in_specs=[in_vmem] * 3,
        out_specs=[in_hbm] * 2,
        out_shape=[jax.ShapeDtypeStruct(signal.shape, signal.dtype)] * 2,
        scratch_shapes=[whole, whole, copy_sems],
        compiler_params=vmem(8),
        name="carry",
    )(both, decay_rate, returned)


def solution(mesh):
    in_specs = (P("seq", "chan"), P("seq", "chan"), P(None, "chan"), P(None, "chan"), P("chan"))
    out_specs = (P("seq", "chan"), P("seq", "chan"))
    return jax.shard_map(
        lambda *arrays: tuple(shards(*arrays)),
        mesh=mesh,
        in_specs=in_specs,
        out_specs=out_specs,
        check_vma=False,
    )
```

```python
import functools
import jax
import jax.numpy as jnp
from jax import lax
from jax.experimental import pallas as pl
from jax.experimental.pallas import tpu as pltpu
from jax.sharding import PartitionSpec as P

SUB = 8
LANES = 128
F32 = jnp.float32
ROOT, ROOT_OF = 41, 64
PARTS = 2


def row_of(table, n):
    return jnp.broadcast_to(table[n : n + 1, :], (SUB, LANES))


def block_index():
    return lax.broadcasted_iota(jnp.int32, (SUB, LANES), 0)


def summed_positions(parts):
    at = block_index()
    low = at < 4
    parts = [
        jnp.where(low, parts[i], parts[i + 4])
        + pltpu.roll(jnp.where(low, parts[i + 4], parts[i]), 4, 0)
        for i in range(4)
    ]
    for by in (2, 1):
        low = lax.rem(at, 2 * by) < by
        parts = [
            jnp.where(
                low,
                parts[i] + pltpu.roll(parts[i], SUB - by, 0),
                parts[i + by] + pltpu.roll(parts[i + by], by, 0),
            )
            for i in range(by)
        ]
    return parts[0]


def ends_kernel(
    signal_hbm,
    cotangent_hbm,
    rate_hbm,
    ends_ref,
    signal_ref,
    cotangent_ref,
    rate_ref,
    sems,
    rate_sem,
):
    positions, width = signal_ref.shape
    states = rate_ref.shape[0]
    tiles = positions // SUB

    def part_copies(part):
        lanes = pl.ds(pl.multiple_of(part * 2 * LANES, 2 * LANES), 2 * LANES)
        return [
            pltpu.make_async_copy(hbm.at[:, lanes], ref.at[:, lanes], sems.at[side, part])
            for side, (hbm, ref) in enumerate(
                ((signal_hbm, signal_ref), (cotangent_hbm, cotangent_ref))
            )
        ]

    rate_copy = pltpu.make_async_copy(rate_hbm, rate_ref, rate_sem)
    rate_copy.start()
    for part in range(width // (2 * LANES)):
        for copy in part_copies(part):
            copy.start()
    rate_copy.wait()
    place = block_index()
    after = (SUB - 1 - place).astype(F32)
    before = place.astype(F32)

    def column(c, _):
        lanes = pl.ds(pl.multiple_of(c * LANES, LANES), LANES)
        rate = rate_ref[:, lanes]
        decay_table = jnp.exp(-rate * float(SUB))
        decay = [row_of(decay_table, n) for n in range(states)]
        ends = [None] * states
        starts = [None] * states
        for pair in range(tiles // 2):
            first = pair * 2 * SUB
            x = signal_ref[first : first + 2 * SUB, lanes].astype(F32)
            last = positions - 2 * SUB - first
            g = cotangent_ref[last : last + 2 * SUB, lanes].astype(F32)
            for half in range(2):
                xh = x[half * SUB : (half + 1) * SUB]
                gh = g[(1 - half) * SUB : (2 - half) * SUB]
                for n in range(states):
                    if pair == 0 and half == 0:
                        ends[n], starts[n] = xh, gh
                    else:
                        ends[n] = decay[n] * ends[n] + xh
                        starts[n] = decay[n] * starts[n] + gh
        for side, (sums, distance) in enumerate(((ends, after), (starts, before))):
            for low in range(0, states, SUB):
                parts = [
                    jnp.exp(-row_of(rate, n) * distance) * sums[n]
                    for n in range(low, low + SUB)
                ]
                at = pl.ds(pl.multiple_of(c * states + low, SUB), SUB)
                ends_ref[side, at, :] = summed_positions(parts)
        return 0

    def both_columns(part, _):
        for copy in part_copies(part):
            copy.wait()
        return lax.fori_loop(2 * part, 2 * part + 2, column, 0)

    lax.fori_loop(0, width // (2 * LANES), both_columns, 0)


def within_kernel(
    is_forward,
    x_hbm,
    rate_hbm,
    weight_hbm,
    gain_hbm,
    *refs,
):
    (
        both_ref,
        span_ref,
        whole_ref,
        turned_ref,
        rate_ref,
        weight_ref,
        gain_ref,
        decays_ref,
        weights_ref,
        gains_ref,
        sems,
        table_sems,
    ) = refs[-12:]
    local_ref = both_ref.at[0 if is_forward else 1]
    positions, width = whole_ref.shape
    states = rate_ref.shape[0]
    columns = width // LANES
    pair = 2 * SUB
    place = block_index()
    distance = (place + 1 if is_forward else SUB - place).astype(F32)

    def part_copy(part):
        rows = pl.ds(part * (positions // PARTS), positions // PARTS)
        return pltpu.make_async_copy(x_hbm.at[rows, :], whole_ref.at[rows, :], sems.at[part])

    table_copies = [
        pltpu.make_async_copy(hbm, ref, table_sems.at[i])
        for i, (hbm, ref) in enumerate(
            ((rate_hbm, rate_ref), (weight_hbm, weight_ref), (gain_hbm, gain_ref))
        )
    ]
    for copy in table_copies:
        copy.start()
    for part in range(PARTS):
        part_copy(part).start()
    for copy in table_copies:
        copy.wait()

    for c in range(columns):
        lanes = pl.ds(c * LANES, LANES)
        rate = rate_ref[:, lanes]
        weight = weight_ref[:, lanes]
        span_ref[pl.ds(c * states, states), :] = jnp.exp(-rate * float(positions))
        decays_ref[pl.ds(c, states, stride=columns), :] = jnp.exp(-rate)
        weights_ref[pl.ds(c, states, stride=columns), :] = weight
        gains_ref[pl.ds(c, 1), :] = gain_ref[:, lanes]
        for n in range(states):
            reach = jnp.exp(-row_of(rate, n) * distance)
            local_ref[pl.ds(positions + n * SUB, SUB), lanes] = row_of(weight, n) * reach
    decay = [decays_ref[n * columns : (n + 1) * columns, :] for n in range(states)]
    weight = [weights_ref[n * columns : (n + 1) * columns, :] for n in range(states)]
    gain = gains_ref[...]
    for part in range(PARTS):
        part_copy(part).wait()

    def advance(step, state):
        at = step if is_forward else positions // pair - 1 - step
        start = pl.multiple_of(at * pair, pair)
        for c in range(columns):
            x = whole_ref[pl.ds(start, pair), c * LANES : (c + 1) * LANES]
            turned_ref[pl.ds(c, pair, stride=columns), :] = x.astype(F32)
        state = list(state)
        for t in range(pair) if is_forward else range(pair - 1, -1, -1):
            x = turned_ref[t * columns : (t + 1) * columns, :]
            terms = [gain * x]
            for n in range(states):
                state[n] = decay[n] * state[n] + x
                terms.append(weight[n] * state[n])
            turned_ref[t * columns : (t + 1) * columns, :] = added(terms)
        for c in range(columns):
            y = turned_ref[pl.ds(c, pair, stride=columns), :]
            local_ref[pl.ds(start, pair), c * LANES : (c + 1) * LANES] = y
        return tuple(state)

    zero = jnp.zeros((columns, LANES), F32)
    lax.fori_loop(0, positions // pair, advance, (zero,) * states)


def added(terms):
    while len(terms) > 1:
        terms = [
            terms[i] + terms[i + 1] if i + 1 < len(terms) else terms[i]
            for i in range(0, len(terms), 2)
        ]
    return terms[0]


def relay_kernel(first, share_ref, ends_ref, span_ref, carried_ref):
    devices, rows, _ = ends_ref.shape
    share = share_ref[0]
    forward = share < devices // 2
    span = span_ref[pl.ds(lax.rem(share, devices // 2) * rows, rows), :]
    state = jnp.zeros(span.shape, F32)
    for step in range(devices):
        ahead, behind = (step - first) % devices, (devices - 1 - step - first) % devices
        at = jnp.where(forward, ahead, behind)
        end = ends_ref[at]
        carried_ref[at] = state
        state = span * state + end


def carry_kernel(
    both_ref, rate_ref, carried_ref, out_hbm, grad_hbm, out_ref, grad_ref, sems
):
    positions, width = out_ref.shape
    states = rate_ref.shape[0]
    tiles = positions // SUB

    def part_copies(part):
        lanes = pl.ds(pl.multiple_of(part * 2 * LANES, 2 * LANES), 2 * LANES)
        return [
            pltpu.make_async_copy(ref.at[:, lanes], hbm.at[:, lanes], sems.at[side, part])
            for side, (hbm, ref) in enumerate(((out_hbm, out_ref), (grad_hbm, grad_ref)))
        ]

    def column(c, _):
        lanes = pl.ds(pl.multiple_of(c * LANES, LANES), LANES)
        decay_table = jnp.exp(-rate_ref[:, lanes] * float(SUB))
        decay = [row_of(decay_table, n) for n in range(states)]
        rows = pl.ds(pl.multiple_of(c * states, states), states)
        for side, result in enumerate((out_ref, grad_ref)):
            local_ref = both_ref.at[side]
            carried = carried_ref[side, rows, :]
            terms = [
                local_ref[pl.ds(positions + n * SUB, SUB), lanes] * row_of(carried, n)
                for n in range(states)
            ]
            for pair in range(tiles // 2):
                halves = []
                first = pair * 2 * SUB if side == 0 else positions - (pair + 1) * 2 * SUB
                for half in range(2):
                    if pair or half:
                        terms = [decay[n] * terms[n] for n in range(states)]
                    start = first + (half if side == 0 else 1 - half) * SUB
                    local = local_ref[pl.ds(start, SUB), lanes]
                    halves.append(added(terms) + local)
                if side:
                    halves.reverse()
                both = jnp.concatenate(halves, axis=0)
                result[first : first + 2 * SUB, lanes] = both.astype(result.dtype)
        return 0

    def both_columns(part, _):
        lax.fori_loop(2 * part, 2 * part + 2, column, 0)
        for copy in part_copies(part):
            copy.start()
        return 0

    lax.fori_loop(0, width // (2 * LANES), both_columns, 0)
    for part in range(width // (2 * LANES)):
        for copy in part_copies(part):
            copy.wait()


def vmem(mib):
    return pltpu.CompilerParams(vmem_limit_bytes=mib << 20)


def shards(signal, cotangent, decay_rate, residue, skip_gain):
    positions, channels = signal.shape
    states = decay_rate.shape[0]
    columns = channels // LANES
    devices = lax.axis_size("seq")
    anywhere = pl.BlockSpec(memory_space=pl.ANY)
    in_hbm = pl.BlockSpec(memory_space=pltpu.HBM)
    in_vmem = pl.BlockSpec(memory_space=pltpu.VMEM)
    elements = positions * channels * states
    whole = pltpu.VMEM((positions, channels), signal.dtype)
    turned = pltpu.VMEM((states * columns, LANES), F32)
    table = pltpu.VMEM(decay_rate.shape, F32)
    copy_sems = pltpu.SemaphoreType.DMA((2, columns // 2))

    ends = pl.pallas_call(
        ends_kernel,
        in_specs=[in_hbm] * 3,
        out_specs=in_vmem,
        out_shape=jax.ShapeDtypeStruct((2, columns * states, LANES), F32),
        scratch_shapes=[
            whole,
            whole,
            table,
            copy_sems,
            pltpu.SemaphoreType.DMA,
        ],
        compiler_params=vmem(56),
        name="ends",
    )(signal, cotangent, decay_rate)

    rows = 2 * columns * states // devices
    sent = ends.reshape(devices, rows, LANES)
    first = ROOT * devices // ROOT_OF
    group = [[(first + i) % devices for i in range(devices)]]
    exchanged = functools.partial(
        lax.all_to_all,
        axis_name="seq",
        split_axis=0,
        concat_axis=0,
        axis_index_groups=group,
    )
    gathered = exchanged(sent)

    weight = residue * jnp.sqrt(-jnp.expm1(-2.0 * decay_rate))
    gain = skip_gain.reshape(1, channels)
    depth = positions + states * SUB

    def within(is_forward, x, *other):
        return pl.pallas_call(
            functools.partial(within_kernel, is_forward),
            in_specs=[in_hbm] * 4 + [in_vmem] * len(other),
            out_specs=[in_vmem] * 2,
            out_shape=[
                jax.ShapeDtypeStruct((2, depth, channels), F32),
                jax.ShapeDtypeStruct((columns * states, LANES), F32),
            ],
            input_output_aliases={4: 0} if other else {},
            scratch_shapes=[
                whole,
                pltpu.VMEM((2 * SUB * columns, LANES), F32),
                table,
                table,
                pltpu.VMEM((1, channels), F32),
                turned,
                turned,
                pltpu.VMEM((columns, LANES), F32),
                pltpu.SemaphoreType.DMA((PARTS,)),
                pltpu.SemaphoreType.DMA((3,)),
            ],
            cost_estimate=pl.CostEstimate(
                flops=6 * elements, bytes_accessed=6 * positions * channels, transcendentals=0
            ),
            compiler_params=vmem(8),
            name="within_forward" if is_forward else "within_backward",
        )(x, decay_rate, weight, gain, *other)

    half, span = within(True, signal)
    both, _ = within(False, cotangent, half)
    share = lax.rem(lax.axis_index("seq") + (devices - first), devices)
    share = share.astype(jnp.int32).reshape(1)
    carried = pl.pallas_call(
        functools.partial(relay_kernel, first),
        in_specs=[pl.BlockSpec(memory_space=pltpu.SMEM), in_vmem, in_vmem],
        out_specs=in_vmem,
        out_shape=jax.ShapeDtypeStruct((devices, rows, LANES), F32),
        compiler_params=vmem(4),
        name="relay",
    )(share, gathered, span)
    returned = exchanged(carried).reshape(2, columns * states, LANES)

    return pl.pallas_call(
        carry_kernel,
        in_specs=[in_vmem] * 3,
        out_specs=[in_hbm] * 2,
        out_shape=[jax.ShapeDtypeStruct(signal.shape, signal.dtype)] * 2,
        scratch_shapes=[whole, whole, copy_sems],
        compiler_params=vmem(8),
        name="carry",
    )(both, decay_rate, returned)


def solution(mesh):
    in_specs = (P("seq", "chan"), P("seq", "chan"), P(None, "chan"), P(None, "chan"), P("chan"))
    out_specs = (P("seq", "chan"), P("seq", "chan"))
    return jax.shard_map(
        lambda *arrays: tuple(shards(*arrays)),
        mesh=mesh,
        in_specs=in_specs,
        out_specs=out_specs,
        check_vma=False,
    )
```

```python
import functools
import jax
import jax.numpy as jnp
from jax import lax
from jax.experimental import pallas as pl
from jax.experimental.pallas import tpu as pltpu
from jax.sharding import PartitionSpec as P

PARTS = 4
SUB = 8
LANES = 128
F32 = jnp.float32


def row_of(table, n):
    return jnp.broadcast_to(table[n : n + 1, :], (SUB, LANES))


def block_index():
    return lax.broadcasted_iota(jnp.int32, (SUB, LANES), 0)


def ends_kernel(
    signal_hbm,
    cotangent_hbm,
    rate_hbm,
    ends_ref,
    signal_ref,
    cotangent_ref,
    rate_ref,
    turned_ref,
    decays_ref,
    sems,
    rate_sem,
):
    positions, width = signal_ref.shape
    states = rate_ref.shape[0]
    columns = width // LANES
    pair = 2 * SUB
    share = positions // PARTS

    def part_copies(part):
        copies = []
        for side, (hbm, ref) in enumerate(
            ((signal_hbm, signal_ref), (cotangent_hbm, cotangent_ref))
        ):
            at = part if side == 0 else PARTS - 1 - part
            rows = pl.ds(pl.multiple_of(at * share, share), share)
            copies.append(
                pltpu.make_async_copy(hbm.at[rows, :], ref.at[rows, :], sems.at[side, part])
            )
        return copies

    rate_copy = pltpu.make_async_copy(rate_hbm, rate_ref, rate_sem)
    rate_copy.start()
    for part in range(PARTS):
        for copy in part_copies(part):
            copy.start()
    rate_copy.wait()
    for c in range(columns):
        rate = rate_ref[:, c * LANES : (c + 1) * LANES]
        decays_ref[pl.ds(c, states, stride=columns), :] = jnp.exp(-rate)
    decay = [decays_ref[n * columns : (n + 1) * columns, :] for n in range(states)]

    def advance(step, state):
        start = pl.multiple_of(step * pair, pair)
        last = pl.multiple_of(positions - pair - step * pair, pair)
        for c in range(columns):
            lanes = pl.ds(c * LANES, LANES)
            x = signal_ref[pl.ds(start, pair), lanes]
            turned_ref[0, pl.ds(c, pair, stride=columns), :] = x.astype(F32)
            g = cotangent_ref[pl.ds(last, pair), lanes]
            turned_ref[1, pl.ds(c, pair, stride=columns), :] = g.astype(F32)
        ends, starts = list(state[0]), list(state[1])
        for t in range(pair):
            x = turned_ref[0, t * columns : (t + 1) * columns, :]
            back = pair - 1 - t
            g = turned_ref[1, back * columns : (back + 1) * columns, :]
            for n in range(states):
                ends[n] = decay[n] * ends[n] + x
                starts[n] = decay[n] * starts[n] + g
        return tuple(ends), tuple(starts)

    def part_of(part, state):
        for copy in part_copies(part):
            copy.wait()
        steps = share // pair
        return lax.fori_loop(part * steps, (part + 1) * steps, advance, state)

    zero = (jnp.zeros((columns, LANES), F32),) * states
    sums = lax.fori_loop(0, PARTS, part_of, (zero, zero))
    for side in range(2):
        for n in range(states):
            ends_ref[side, n * columns : (n + 1) * columns, :] = sums[side][n]


def within_kernel(is_forward, x_ref, table_ref, *refs):
    both_ref, turned_ref, decays_ref, weights_ref, gains_ref = refs[-5:]
    local_ref = both_ref.at[0 if is_forward else 1]
    positions, width = x_ref.shape
    states = (table_ref.shape[0] - 1) // 2
    columns = width // LANES
    pair = 2 * SUB
    place = block_index()
    distance = (place + 1 if is_forward else SUB - place).astype(F32)

    for c in range(columns):
        lanes = pl.ds(c * LANES, LANES)
        rate = table_ref[:states, lanes]
        weight = table_ref[states : 2 * states, lanes]
        decays_ref[pl.ds(c, states, stride=columns), :] = jnp.exp(-rate)
        weights_ref[pl.ds(c, states, stride=columns), :] = weight
        gains_ref[pl.ds(c, 1), :] = table_ref[2 * states :, lanes]
        for n in range(states):
            reach = jnp.exp(-row_of(rate, n) * distance)
            local_ref[pl.ds(positions + n * SUB, SUB), lanes] = row_of(weight, n) * reach
    decay = [decays_ref[n * columns : (n + 1) * columns, :] for n in range(states)]
    weight = [weights_ref[n * columns : (n + 1) * columns, :] for n in range(states)]
    gain = gains_ref[...]

    def advance(step, state):
        at = step if is_forward else positions // pair - 1 - step
        start = pl.multiple_of(at * pair, pair)
        for c in range(columns):
            x = x_ref[pl.ds(start, pair), c * LANES : (c + 1) * LANES]
            turned_ref[pl.ds(c, pair, stride=columns), :] = x.astype(F32)
        state = list(state)
        for t in range(pair) if is_forward else range(pair - 1, -1, -1):
            x = turned_ref[t * columns : (t + 1) * columns, :]
            terms = [gain * x]
            for n in range(states):
                state[n] = decay[n] * state[n] + x
                terms.append(weight[n] * state[n])
            turned_ref[t * columns : (t + 1) * columns, :] = added(terms)
        for c in range(columns):
            y = turned_ref[pl.ds(c, pair, stride=columns), :]
            local_ref[pl.ds(start, pair), c * LANES : (c + 1) * LANES] = y
        return tuple(state)

    zero = jnp.zeros((columns, LANES), F32)
    lax.fori_loop(0, positions // pair, advance, (zero,) * states)


def added(terms):
    while len(terms) > 1:
        terms = [
            terms[i] + terms[i + 1] if i + 1 < len(terms) else terms[i]
            for i in range(0, len(terms), 2)
        ]
    return terms[0]


class Layout:
    def __init__(self, devices):
        self.lows = 4
        self.lines = max(2, devices // 16)
        self.highs = devices // (self.lows * self.lines)
        self.members = self.lines * self.lows
        self.middle = self.highs // 2
        self.first = self.lines // 2 * self.lows + 1


    def member_groups(self):
        return [
            [
                m // self.lows * self.highs * self.lows + high * self.lows + m % self.lows
                for m in ((self.first + i) % self.members for i in range(self.members))
            ]
            for high in range(self.highs)
        ]

    def peer_groups(self):
        return [
            [
                (line * self.highs + (self.middle + i) % self.highs) * self.lows + low
                for i in range(self.highs)
            ]
            for line in range(self.lines)
            for low in range(self.lows)
        ]

    def place(self, index):
        high = lax.rem(index // self.lows, self.highs)
        line = index // (self.lows * self.highs)
        return high, self.slot(line, lax.rem(index, self.lows))

    def slot(self, line, low):
        member = line * self.lows + low
        return lax.rem(member + (self.members - self.first), self.members)


def share_of(layout, index_ref, span_ref, rows):
    high, share = layout.place(index_ref[0])
    half = layout.members // 2
    at = pl.multiple_of(lax.rem(share, half) * rows, rows)
    return high, share < half, span_ref[pl.ds(at, rows), :]


def totals_kernel(layout, index_ref, ends_ref, span_ref, totals_ref):
    rows = ends_ref.shape[1]
    _, forward, span = share_of(layout, index_ref, span_ref, rows)
    for line in range(layout.lines):
        total = None
        for step in range(layout.lows):
            low = jnp.where(forward, step, layout.lows - 1 - step)
            end = ends_ref[layout.slot(line, low)]
            total = end if total is None else span * total + end
        for peer in range(layout.highs):
            totals_ref[peer, line] = total


def relay_kernel(layout, index_ref, ends_ref, totals_ref, span_ref, carried_ref):
    rows = ends_ref.shape[1]
    high, forward, span = share_of(layout, index_ref, span_ref, rows)
    stride = span
    for _ in range(layout.lows - 1):
        stride = stride * span
    state = jnp.zeros(span.shape, F32)
    for line_step in range(layout.lines):
        line = jnp.where(forward, line_step, layout.lines - 1 - line_step)
        entering = state
        for high_step in range(layout.highs):
            this = jnp.where(forward, high_step, layout.highs - 1 - high_step)
            entering = jnp.where(this == high, state, entering)
            peer = lax.rem(this + layout.highs - layout.middle, layout.highs)
            state = stride * state + totals_ref[peer, line]
        for step in range(layout.lows):
            low = jnp.where(forward, step, layout.lows - 1 - step)
            at = layout.slot(line, low)
            carried_ref[at] = entering
            entering = span * entering + ends_ref[at]


def carry_kernel(
    both_ref, rate_ref, carried_ref, out_hbm, grad_hbm, out_ref, grad_ref, sems
):
    positions, width = out_ref.shape
    states = rate_ref.shape[0]
    tiles = positions // SUB

    def part_copies(part):
        lanes = pl.ds(pl.multiple_of(part * 2 * LANES, 2 * LANES), 2 * LANES)
        return [
            pltpu.make_async_copy(ref.at[:, lanes], hbm.at[:, lanes], sems.at[side, part])
            for side, (hbm, ref) in enumerate(((out_hbm, out_ref), (grad_hbm, grad_ref)))
        ]

    def column(c, _):
        lanes = pl.ds(pl.multiple_of(c * LANES, LANES), LANES)
        decay_table = jnp.exp(-rate_ref[:, lanes] * float(SUB))
        decay = [row_of(decay_table, n) for n in range(states)]
        rows = pl.ds(c, states, stride=width // LANES)
        for side, result in enumerate((out_ref, grad_ref)):
            local_ref = both_ref.at[side]
            carried = carried_ref[side, rows, :]
            terms = [
                local_ref[pl.ds(positions + n * SUB, SUB), lanes] * row_of(carried, n)
                for n in range(states)
            ]
            for pair in range(tiles // 2):
                halves = []
                first = pair * 2 * SUB if side == 0 else positions - (pair + 1) * 2 * SUB
                for half in range(2):
                    if pair or half:
                        terms = [decay[n] * terms[n] for n in range(states)]
                    start = first + (half if side == 0 else 1 - half) * SUB
                    local = local_ref[pl.ds(start, SUB), lanes]
                    halves.append(added(terms) + local)
                if side:
                    halves.reverse()
                both = jnp.concatenate(halves, axis=0)
                result[first : first + 2 * SUB, lanes] = both.astype(result.dtype)
        return 0

    def both_columns(part, _):
        lax.fori_loop(2 * part, 2 * part + 2, column, 0)
        for copy in part_copies(part):
            copy.start()
        return 0

    lax.fori_loop(0, width // (2 * LANES), both_columns, 0)
    for part in range(width // (2 * LANES)):
        for copy in part_copies(part):
            copy.wait()


def vmem(mib):
    return pltpu.CompilerParams(vmem_limit_bytes=mib << 20)


def shards(signal, cotangent, decay_rate, residue, skip_gain):
    positions, channels = signal.shape
    states = decay_rate.shape[0]
    columns = channels // LANES
    devices = lax.axis_size("seq")
    anywhere = pl.BlockSpec(memory_space=pl.ANY)
    in_hbm = pl.BlockSpec(memory_space=pltpu.HBM)
    in_vmem = pl.BlockSpec(memory_space=pltpu.VMEM)
    elements = positions * channels * states
    whole = pltpu.VMEM((positions, channels), signal.dtype)
    turned = pltpu.VMEM((states * columns, LANES), F32)
    copy_sems = pltpu.SemaphoreType.DMA((2, columns // 2))

    ends = pl.pallas_call(
        ends_kernel,
        in_specs=[in_hbm] * 3,
        out_specs=in_vmem,
        out_shape=jax.ShapeDtypeStruct((2, columns * states, LANES), F32),
        scratch_shapes=[
            whole,
            whole,
            pltpu.VMEM(decay_rate.shape, F32),
            pltpu.VMEM((2, 2 * SUB * columns, LANES), F32),
            turned,
            pltpu.SemaphoreType.DMA((2, PARTS)),
            pltpu.SemaphoreType.DMA,
        ],
        compiler_params=vmem(56),
        name="ends",
    )(signal, cotangent, decay_rate)

    layout = Layout(devices)
    rows = 2 * columns * states // layout.members
    index = lax.axis_index("seq").astype(jnp.int32).reshape(1)
    in_smem = pl.BlockSpec(memory_space=pltpu.SMEM)

    def exchanged(x, groups):
        return lax.all_to_all(x, "seq", 0, 0, axis_index_groups=groups)

    gathered = exchanged(ends.reshape(layout.members, rows, LANES), layout.member_groups())
    rate_then, _ = lax.optimization_barrier((decay_rate, ends))
    span = jnp.exp(-float(positions) * rate_then).reshape(states * columns, LANES)
    weight = residue * jnp.sqrt(-jnp.expm1(-2.0 * rate_then))
    tables = jnp.concatenate([rate_then, weight, skip_gain.reshape(1, channels)], axis=0)
    span, tables = lax.optimization_barrier((span, tables))
    totals = pl.pallas_call(
        functools.partial(totals_kernel, layout),
        in_specs=[in_smem, in_vmem, in_vmem],
        out_specs=in_vmem,
        out_shape=jax.ShapeDtypeStruct((layout.highs, layout.lines, rows, LANES), F32),
        compiler_params=vmem(4),
        name="totals",
    )(index, gathered, span)
    peers = exchanged(totals, layout.peer_groups())

    depth = positions + states * SUB

    def within(is_forward, x, *other):
        return pl.pallas_call(
            functools.partial(within_kernel, is_forward),
            in_specs=[in_vmem] * (2 + len(other)),
            out_specs=in_vmem,
            out_shape=jax.ShapeDtypeStruct((2, depth, channels), F32),
            input_output_aliases={2: 0} if other else {},
            scratch_shapes=[
                pltpu.VMEM((2 * SUB * columns, LANES), F32),
                turned,
                turned,
                pltpu.VMEM((columns, LANES), F32),
            ],
            cost_estimate=pl.CostEstimate(
                flops=6 * elements, bytes_accessed=6 * positions * channels, transcendentals=0
            ),
            compiler_params=vmem(8),
            name="within_forward" if is_forward else "within_backward",
        )(x, tables, *other)

    signal, _ = lax.optimization_barrier((signal, totals))
    half = within(True, signal)
    span, half = lax.optimization_barrier((span, half))

    carried = pl.pallas_call(
        functools.partial(relay_kernel, layout),
        in_specs=[in_smem] + [in_vmem] * 3,
        out_specs=in_vmem,
        out_shape=jax.ShapeDtypeStruct((layout.members, rows, LANES), F32),
        compiler_params=vmem(56),
        name="relay",
    )(index, gathered, peers, span)
    cotangent, _ = lax.optimization_barrier((cotangent, carried))
    both = within(False, cotangent, half)
    returned = exchanged(carried, layout.member_groups())
    returned = returned.reshape(2, columns * states, LANES)

    return pl.pallas_call(
        carry_kernel,
        in_specs=[in_vmem] * 3,
        out_specs=[in_hbm] * 2,
        out_shape=[jax.ShapeDtypeStruct(signal.shape, signal.dtype)] * 2,
        scratch_shapes=[whole, whole, copy_sems],
        compiler_params=vmem(8),
        name="carry",
    )(both, decay_rate, returned)


def solution(mesh):
    in_specs = (P("seq", "chan"), P("seq", "chan"), P(None, "chan"), P(None, "chan"), P("chan"))
    out_specs = (P("seq", "chan"), P("seq", "chan"))
    return jax.shard_map(
        lambda *arrays: tuple(shards(*arrays)),
        mesh=mesh,
        in_specs=in_specs,
        out_specs=out_specs,
        check_vma=False,
    )
```

```python
import functools
import jax
import jax.numpy as jnp
from jax import lax
from jax.experimental import pallas as pl
from jax.experimental.pallas import tpu as pltpu
from jax.sharding import PartitionSpec as P

SUB = 8
LANES = 128
F32 = jnp.float32


def row_of(table, n):
    return jnp.broadcast_to(table[n : n + 1, :], (SUB, LANES))


def block_index():
    return lax.broadcasted_iota(jnp.int32, (SUB, LANES), 0)


def summed_positions(parts):
    at = block_index()
    low = at < 4
    parts = [
        jnp.where(low, parts[i], parts[i + 4])
        + pltpu.roll(jnp.where(low, parts[i + 4], parts[i]), 4, 0)
        for i in range(4)
    ]
    for by in (2, 1):
        low = lax.rem(at, 2 * by) < by
        parts = [
            jnp.where(
                low,
                parts[i] + pltpu.roll(parts[i], SUB - by, 0),
                parts[i + by] + pltpu.roll(parts[i + by], by, 0),
            )
            for i in range(by)
        ]
    return parts[0]


def ends_kernel(
    signal_hbm,
    cotangent_hbm,
    rate_hbm,
    ends_ref,
    signal_ref,
    cotangent_ref,
    rate_ref,
    sems,
    rate_sem,
):
    positions, width = signal_ref.shape
    states = rate_ref.shape[0]
    tiles = positions // SUB

    def part_copies(part):
        lanes = pl.ds(pl.multiple_of(part * 2 * LANES, 2 * LANES), 2 * LANES)
        return [
            pltpu.make_async_copy(hbm.at[:, lanes], ref.at[:, lanes], sems.at[side, part])
            for side, (hbm, ref) in enumerate(
                ((signal_hbm, signal_ref), (cotangent_hbm, cotangent_ref))
            )
        ]

    rate_copy = pltpu.make_async_copy(rate_hbm, rate_ref, rate_sem)
    rate_copy.start()
    for part in range(width // (2 * LANES)):
        for copy in part_copies(part):
            copy.start()
    rate_copy.wait()
    place = block_index()
    after = (SUB - 1 - place).astype(F32)
    before = place.astype(F32)

    def column(c, _):
        lanes = pl.ds(pl.multiple_of(c * LANES, LANES), LANES)
        rate = rate_ref[:, lanes]
        decay_table = jnp.exp(-rate * float(SUB))
        decay = [row_of(decay_table, n) for n in range(states)]
        ends = [None] * states
        starts = [None] * states
        for pair in range(tiles // 2):
            first = pair * 2 * SUB
            x = signal_ref[first : first + 2 * SUB, lanes].astype(F32)
            last = positions - 2 * SUB - first
            g = cotangent_ref[last : last + 2 * SUB, lanes].astype(F32)
            for half in range(2):
                xh = x[half * SUB : (half + 1) * SUB]
                gh = g[(1 - half) * SUB : (2 - half) * SUB]
                for n in range(states):
                    if pair == 0 and half == 0:
                        ends[n], starts[n] = xh, gh
                    else:
                        ends[n] = decay[n] * ends[n] + xh
                        starts[n] = decay[n] * starts[n] + gh
        for side, (sums, distance) in enumerate(((ends, after), (starts, before))):
            for low in range(0, states, SUB):
                parts = [
                    jnp.exp(-row_of(rate, n) * distance) * sums[n]
                    for n in range(low, low + SUB)
                ]
                at = pl.ds(pl.multiple_of(c * states + low, SUB), SUB)
                ends_ref[side, at, :] = summed_positions(parts)
        return 0

    def both_columns(part, _):
        for copy in part_copies(part):
            copy.wait()
        return lax.fori_loop(2 * part, 2 * part + 2, column, 0)

    lax.fori_loop(0, width // (2 * LANES), both_columns, 0)


def within_kernel(is_forward, x_ref, table_ref, *refs):
    both_ref, turned_ref, decays_ref, weights_ref, gains_ref = refs[-5:]
    local_ref = both_ref.at[0 if is_forward else 1]
    positions, width = x_ref.shape
    states = (table_ref.shape[0] - 1) // 2
    columns = width // LANES
    pair = 2 * SUB
    place = block_index()
    distance = (place + 1 if is_forward else SUB - place).astype(F32)

    for c in range(columns):
        lanes = pl.ds(c * LANES, LANES)
        rate = table_ref[:states, lanes]
        weight = table_ref[states : 2 * states, lanes]
        decays_ref[pl.ds(c, states, stride=columns), :] = jnp.exp(-rate)
        weights_ref[pl.ds(c, states, stride=columns), :] = weight
        gains_ref[pl.ds(c, 1), :] = table_ref[2 * states :, lanes]
        for n in range(states):
            reach = jnp.exp(-row_of(rate, n) * distance)
            local_ref[pl.ds(positions + n * SUB, SUB), lanes] = row_of(weight, n) * reach
    decay = [decays_ref[n * columns : (n + 1) * columns, :] for n in range(states)]
    weight = [weights_ref[n * columns : (n + 1) * columns, :] for n in range(states)]
    gain = gains_ref[...]

    def advance(step, state):
        at = step if is_forward else positions // pair - 1 - step
        start = pl.multiple_of(at * pair, pair)
        for c in range(columns):
            x = x_ref[pl.ds(start, pair), c * LANES : (c + 1) * LANES]
            turned_ref[pl.ds(c, pair, stride=columns), :] = x.astype(F32)
        state = list(state)
        for t in range(pair) if is_forward else range(pair - 1, -1, -1):
            x = turned_ref[t * columns : (t + 1) * columns, :]
            terms = [gain * x]
            for n in range(states):
                state[n] = decay[n] * state[n] + x
                terms.append(weight[n] * state[n])
            turned_ref[t * columns : (t + 1) * columns, :] = added(terms)
        for c in range(columns):
            y = turned_ref[pl.ds(c, pair, stride=columns), :]
            local_ref[pl.ds(start, pair), c * LANES : (c + 1) * LANES] = y
        return tuple(state)

    zero = jnp.zeros((columns, LANES), F32)
    lax.fori_loop(0, positions // pair, advance, (zero,) * states)


def added(terms):
    while len(terms) > 1:
        terms = [
            terms[i] + terms[i + 1] if i + 1 < len(terms) else terms[i]
            for i in range(0, len(terms), 2)
        ]
    return terms[0]


class Layout:
    def __init__(self, devices):
        self.lows = 4
        self.lines = max(2, devices // 16)
        self.highs = devices // (self.lows * self.lines)
        self.members = self.lines * self.lows
        self.middle = self.highs // 2
        self.first = self.lines // 2 * self.lows + 1


    def member_groups(self):
        return [
            [
                m // self.lows * self.highs * self.lows + high * self.lows + m % self.lows
                for m in ((self.first + i) % self.members for i in range(self.members))
            ]
            for high in range(self.highs)
        ]

    def peer_groups(self):
        return [
            [
                (line * self.highs + (self.middle + i) % self.highs) * self.lows + low
                for i in range(self.highs)
            ]
            for line in range(self.lines)
            for low in range(self.lows)
        ]

    def place(self, index):
        high = lax.rem(index // self.lows, self.highs)
        line = index // (self.lows * self.highs)
        return high, self.slot(line, lax.rem(index, self.lows))

    def slot(self, line, low):
        member = line * self.lows + low
        return lax.rem(member + (self.members - self.first), self.members)


def share_of(layout, index_ref, span_ref, rows):
    high, share = layout.place(index_ref[0])
    half = layout.members // 2
    at = pl.multiple_of(lax.rem(share, half) * rows, rows)
    return high, share < half, span_ref[pl.ds(at, rows), :]


def totals_kernel(layout, index_ref, ends_ref, span_ref, totals_ref):
    rows = ends_ref.shape[1]
    _, forward, span = share_of(layout, index_ref, span_ref, rows)
    for line in range(layout.lines):
        total = None
        for step in range(layout.lows):
            low = jnp.where(forward, step, layout.lows - 1 - step)
            end = ends_ref[layout.slot(line, low)]
            total = end if total is None else span * total + end
        for peer in range(layout.highs):
            totals_ref[peer, line] = total


def relay_kernel(layout, index_ref, ends_ref, totals_ref, span_ref, carried_ref):
    rows = ends_ref.shape[1]
    high, forward, span = share_of(layout, index_ref, span_ref, rows)
    stride = span
    for _ in range(layout.lows - 1):
        stride = stride * span
    state = jnp.zeros(span.shape, F32)
    for line_step in range(layout.lines):
        line = jnp.where(forward, line_step, layout.lines - 1 - line_step)
        entering = state
        for high_step in range(layout.highs):
            this = jnp.where(forward, high_step, layout.highs - 1 - high_step)
            entering = jnp.where(this == high, state, entering)
            peer = lax.rem(this + layout.highs - layout.middle, layout.highs)
            state = stride * state + totals_ref[peer, line]
        for step in range(layout.lows):
            low = jnp.where(forward, step, layout.lows - 1 - step)
            at = layout.slot(line, low)
            carried_ref[at] = entering
            entering = span * entering + ends_ref[at]


def carry_kernel(
    both_ref, rate_ref, carried_ref, out_hbm, grad_hbm, out_ref, grad_ref, sems
):
    positions, width = out_ref.shape
    states = rate_ref.shape[0]
    tiles = positions // SUB

    def part_copies(part):
        lanes = pl.ds(pl.multiple_of(part * 2 * LANES, 2 * LANES), 2 * LANES)
        return [
            pltpu.make_async_copy(ref.at[:, lanes], hbm.at[:, lanes], sems.at[side, part])
            for side, (hbm, ref) in enumerate(((out_hbm, out_ref), (grad_hbm, grad_ref)))
        ]

    def column(c, _):
        lanes = pl.ds(pl.multiple_of(c * LANES, LANES), LANES)
        decay_table = jnp.exp(-rate_ref[:, lanes] * float(SUB))
        decay = [row_of(decay_table, n) for n in range(states)]
        rows = pl.ds(pl.multiple_of(c * states, states), states)
        for side, result in enumerate((out_ref, grad_ref)):
            local_ref = both_ref.at[side]
            carried = carried_ref[side, rows, :]
            terms = [
                local_ref[pl.ds(positions + n * SUB, SUB), lanes] * row_of(carried, n)
                for n in range(states)
            ]
            for pair in range(tiles // 2):
                halves = []
                first = pair * 2 * SUB if side == 0 else positions - (pair + 1) * 2 * SUB
                for half in range(2):
                    if pair or half:
                        terms = [decay[n] * terms[n] for n in range(states)]
                    start = first + (half if side == 0 else 1 - half) * SUB
                    local = local_ref[pl.ds(start, SUB), lanes]
                    halves.append(added(terms) + local)
                if side:
                    halves.reverse()
                both = jnp.concatenate(halves, axis=0)
                result[first : first + 2 * SUB, lanes] = both.astype(result.dtype)
        return 0

    def both_columns(part, _):
        lax.fori_loop(2 * part, 2 * part + 2, column, 0)
        for copy in part_copies(part):
            copy.start()
        return 0

    lax.fori_loop(0, width // (2 * LANES), both_columns, 0)
    for part in range(width // (2 * LANES)):
        for copy in part_copies(part):
            copy.wait()


def vmem(mib):
    return pltpu.CompilerParams(vmem_limit_bytes=mib << 20)


def shards(signal, cotangent, decay_rate, residue, skip_gain):
    positions, channels = signal.shape
    states = decay_rate.shape[0]
    columns = channels // LANES
    devices = lax.axis_size("seq")
    anywhere = pl.BlockSpec(memory_space=pl.ANY)
    in_hbm = pl.BlockSpec(memory_space=pltpu.HBM)
    in_vmem = pl.BlockSpec(memory_space=pltpu.VMEM)
    elements = positions * channels * states
    whole = pltpu.VMEM((positions, channels), signal.dtype)
    turned = pltpu.VMEM((states * columns, LANES), F32)
    copy_sems = pltpu.SemaphoreType.DMA((2, columns // 2))

    ends = pl.pallas_call(
        ends_kernel,
        in_specs=[in_hbm] * 3,
        out_specs=in_vmem,
        out_shape=jax.ShapeDtypeStruct((2, columns * states, LANES), F32),
        scratch_shapes=[
            whole,
            whole,
            pltpu.VMEM(decay_rate.shape, F32),
            copy_sems,
            pltpu.SemaphoreType.DMA,
        ],
        compiler_params=vmem(56),
        name="ends",
    )(signal, cotangent, decay_rate)

    layout = Layout(devices)
    rows = 2 * columns * states // layout.members
    index = lax.axis_index("seq").astype(jnp.int32).reshape(1)
    in_smem = pl.BlockSpec(memory_space=pltpu.SMEM)

    def exchanged(x, groups):
        return lax.all_to_all(x, "seq", 0, 0, axis_index_groups=groups)

    gathered = exchanged(ends.reshape(layout.members, rows, LANES), layout.member_groups())
    rate_then, _ = lax.optimization_barrier((decay_rate, ends))
    span = jnp.exp(-float(positions) * rate_then).reshape(states, columns, LANES)
    span = span.swapaxes(0, 1).reshape(columns * states, LANES)
    weight = residue * jnp.sqrt(-jnp.expm1(-2.0 * rate_then))
    tables = jnp.concatenate([rate_then, weight, skip_gain.reshape(1, channels)], axis=0)
    span, tables = lax.optimization_barrier((span, tables))
    totals = pl.pallas_call(
        functools.partial(totals_kernel, layout),
        in_specs=[in_smem, in_vmem, in_vmem],
        out_specs=in_vmem,
        out_shape=jax.ShapeDtypeStruct((layout.highs, layout.lines, rows, LANES), F32),
        compiler_params=vmem(4),
        name="totals",
    )(index, gathered, span)
    peers = exchanged(totals, layout.peer_groups())

    depth = positions + states * SUB

    def within(is_forward, x, *other):
        return pl.pallas_call(
            functools.partial(within_kernel, is_forward),
            in_specs=[in_vmem] * (2 + len(other)),
            out_specs=in_vmem,
            out_shape=jax.ShapeDtypeStruct((2, depth, channels), F32),
            input_output_aliases={2: 0} if other else {},
            scratch_shapes=[
                pltpu.VMEM((2 * SUB * columns, LANES), F32),
                turned,
                turned,
                pltpu.VMEM((columns, LANES), F32),
            ],
            cost_estimate=pl.CostEstimate(
                flops=6 * elements, bytes_accessed=6 * positions * channels, transcendentals=0
            ),
            compiler_params=vmem(8),
            name="within_forward" if is_forward else "within_backward",
        )(x, tables, *other)

    signal, _ = lax.optimization_barrier((signal, totals))
    half = within(True, signal)
    span, half = lax.optimization_barrier((span, half))

    carried = pl.pallas_call(
        functools.partial(relay_kernel, layout),
        in_specs=[in_smem] + [in_vmem] * 3,
        out_specs=in_vmem,
        out_shape=jax.ShapeDtypeStruct((layout.members, rows, LANES), F32),
        compiler_params=vmem(4),
        name="relay",
    )(index, gathered, peers, span)
    cotangent, _ = lax.optimization_barrier((cotangent, carried))
    both = within(False, cotangent, half)
    returned = exchanged(carried, layout.member_groups())
    returned = returned.reshape(2, columns * states, LANES)

    return pl.pallas_call(
        carry_kernel,
        in_specs=[in_vmem] * 3,
        out_specs=[in_hbm] * 2,
        out_shape=[jax.ShapeDtypeStruct(signal.shape, signal.dtype)] * 2,
        scratch_shapes=[whole, whole, copy_sems],
        compiler_params=vmem(8),
        name="carry",
    )(both, decay_rate, returned)


def solution(mesh):
    in_specs = (P("seq", "chan"), P("seq", "chan"), P(None, "chan"), P(None, "chan"), P("chan"))
    out_specs = (P("seq", "chan"), P("seq", "chan"))
    return jax.shard_map(
        lambda *arrays: tuple(shards(*arrays)),
        mesh=mesh,
        in_specs=in_specs,
        out_specs=out_specs,
        check_vma=False,
    )
```

```python
import functools
import jax
import jax.numpy as jnp
from jax import lax
from jax.experimental import pallas as pl
from jax.experimental.pallas import tpu as pltpu
from jax.sharding import PartitionSpec as P

SUB = 8
LANES = 128
F32 = jnp.float32


def row_of(table, n):
    return jnp.broadcast_to(table[n : n + 1, :], (SUB, LANES))


def block_index():
    return lax.broadcasted_iota(jnp.int32, (SUB, LANES), 0)


def summed_positions(parts):
    at = block_index()
    low = at < 4
    parts = [
        jnp.where(low, parts[i], parts[i + 4])
        + pltpu.roll(jnp.where(low, parts[i + 4], parts[i]), 4, 0)
        for i in range(4)
    ]
    for by in (2, 1):
        low = lax.rem(at, 2 * by) < by
        parts = [
            jnp.where(
                low,
                parts[i] + pltpu.roll(parts[i], SUB - by, 0),
                parts[i + by] + pltpu.roll(parts[i + by], by, 0),
            )
            for i in range(by)
        ]
    return parts[0]


def ends_kernel(
    signal_hbm,
    cotangent_hbm,
    rate_hbm,
    ends_ref,
    signal_ref,
    cotangent_ref,
    rate_ref,
    sems,
    rate_sem,
):
    positions, width = signal_ref.shape
    states = rate_ref.shape[0]
    tiles = positions // SUB

    def part_copies(part):
        lanes = pl.ds(pl.multiple_of(part * 2 * LANES, 2 * LANES), 2 * LANES)
        return [
            pltpu.make_async_copy(hbm.at[:, lanes], ref.at[:, lanes], sems.at[side, part])
            for side, (hbm, ref) in enumerate(
                ((signal_hbm, signal_ref), (cotangent_hbm, cotangent_ref))
            )
        ]

    rate_copy = pltpu.make_async_copy(rate_hbm, rate_ref, rate_sem)
    rate_copy.start()
    for part in range(width // (2 * LANES)):
        for copy in part_copies(part):
            copy.start()
    rate_copy.wait()
    place = block_index()
    after = (SUB - 1 - place).astype(F32)
    before = place.astype(F32)

    def column(c, _):
        lanes = pl.ds(pl.multiple_of(c * LANES, LANES), LANES)
        rate = rate_ref[:, lanes]
        decay_table = jnp.exp(-rate * float(SUB))
        decay = [row_of(decay_table, n) for n in range(states)]
        ends = [None] * states
        starts = [None] * states
        for pair in range(tiles // 2):
            first = pair * 2 * SUB
            x = signal_ref[first : first + 2 * SUB, lanes].astype(F32)
            last = positions - 2 * SUB - first
            g = cotangent_ref[last : last + 2 * SUB, lanes].astype(F32)
            for half in range(2):
                xh = x[half * SUB : (half + 1) * SUB]
                gh = g[(1 - half) * SUB : (2 - half) * SUB]
                for n in range(states):
                    if pair == 0 and half == 0:
                        ends[n], starts[n] = xh, gh
                    else:
                        ends[n] = decay[n] * ends[n] + xh
                        starts[n] = decay[n] * starts[n] + gh
        for side, (sums, distance) in enumerate(((ends, after), (starts, before))):
            for low in range(0, states, SUB):
                parts = [
                    jnp.exp(-row_of(rate, n) * distance) * sums[n]
                    for n in range(low, low + SUB)
                ]
                at = pl.ds(pl.multiple_of(c * states + low, SUB), SUB)
                ends_ref[side, at, :] = summed_positions(parts)
        return 0

    def both_columns(part, _):
        for copy in part_copies(part):
            copy.wait()
        return lax.fori_loop(2 * part, 2 * part + 2, column, 0)

    lax.fori_loop(0, width // (2 * LANES), both_columns, 0)


def within_kernel(is_forward, x_ref, table_ref, *refs):
    both_ref, turned_ref, decays_ref, weights_ref, gains_ref = refs[-5:]
    local_ref = both_ref.at[0 if is_forward else 1]
    positions, width = x_ref.shape
    states = (table_ref.shape[0] - 1) // 2
    columns = width // LANES
    pair = 2 * SUB
    place = block_index()
    distance = (place + 1 if is_forward else SUB - place).astype(F32)

    for c in range(columns):
        lanes = pl.ds(c * LANES, LANES)
        rate = table_ref[:states, lanes]
        weight = table_ref[states : 2 * states, lanes]
        decays_ref[pl.ds(c, states, stride=columns), :] = jnp.exp(-rate)
        weights_ref[pl.ds(c, states, stride=columns), :] = weight
        gains_ref[pl.ds(c, 1), :] = table_ref[2 * states :, lanes]
        for n in range(states):
            reach = jnp.exp(-row_of(rate, n) * distance)
            local_ref[pl.ds(positions + n * SUB, SUB), lanes] = row_of(weight, n) * reach
    decay = [decays_ref[n * columns : (n + 1) * columns, :] for n in range(states)]
    weight = [weights_ref[n * columns : (n + 1) * columns, :] for n in range(states)]
    gain = gains_ref[:columns]

    def advance(step, state):
        at = step if is_forward else positions // pair - 1 - step
        start = pl.multiple_of(at * pair, pair)
        for c in range(columns):
            x = x_ref[pl.ds(start, pair), c * LANES : (c + 1) * LANES]
            turned_ref[pl.ds(c, pair, stride=columns), :] = x.astype(F32)
        state = list(state)
        for t in range(pair) if is_forward else range(pair - 1, -1, -1):
            x = turned_ref[t * columns : (t + 1) * columns, :]
            terms = [gain * x]
            for n in range(states):
                state[n] = decay[n] * state[n] + x
                terms.append(weight[n] * state[n])
            turned_ref[t * columns : (t + 1) * columns, :] = added(terms)
        for c in range(columns):
            y = turned_ref[pl.ds(c, pair, stride=columns), :]
            local_ref[pl.ds(start, pair), c * LANES : (c + 1) * LANES] = y
        return tuple(state)

    zero = jnp.zeros((columns, LANES), F32)
    lax.fori_loop(0, positions // pair, advance, (zero,) * states)


def added(terms):
    while len(terms) > 1:
        terms = [
            terms[i] + terms[i + 1] if i + 1 < len(terms) else terms[i]
            for i in range(0, len(terms), 2)
        ]
    return terms[0]


class Layout:
    def __init__(self, devices):
        self.lows = 4
        self.lines = max(2, devices // 16)
        self.highs = devices // (self.lows * self.lines)
        self.members = self.lines * self.lows
        self.middle = self.highs // 2
        self.first = self.lines // 2 * self.lows + 1


    def member_groups(self):
        return [
            [
                m // self.lows * self.highs * self.lows + high * self.lows + m % self.lows
                for m in ((self.first + i) % self.members for i in range(self.members))
            ]
            for high in range(self.highs)
        ]

    def peer_groups(self):
        return [
            [
                (line * self.highs + (self.middle + i) % self.highs) * self.lows + low
                for i in range(self.highs)
            ]
            for line in range(self.lines)
            for low in range(self.lows)
        ]

    def place(self, index):
        high = lax.rem(index // self.lows, self.highs)
        line = index // (self.lows * self.highs)
        return high, self.slot(line, lax.rem(index, self.lows))

    def slot(self, line, low):
        member = line * self.lows + low
        return lax.rem(member + (self.members - self.first), self.members)


def share_of(layout, index_ref, span_ref, rows):
    high, share = layout.place(index_ref[0])
    half = layout.members // 2
    at = pl.multiple_of(lax.rem(share, half) * rows, rows)
    return high, share < half, span_ref[pl.ds(at, rows), :]


def totals_kernel(layout, index_ref, ends_ref, span_ref, totals_ref):
    rows = ends_ref.shape[1]
    _, forward, span = share_of(layout, index_ref, span_ref, rows)
    for line in range(layout.lines):
        total = None
        for step in range(layout.lows):
            low = jnp.where(forward, step, layout.lows - 1 - step)
            end = ends_ref[layout.slot(line, low)]
            total = end if total is None else span * total + end
        for peer in range(layout.highs):
            totals_ref[peer, line] = total


def relay_kernel(layout, index_ref, ends_ref, totals_ref, span_ref, carried_ref):
    rows = ends_ref.shape[1]
    high, forward, span = share_of(layout, index_ref, span_ref, rows)
    stride = span
    for _ in range(layout.lows - 1):
        stride = stride * span
    state = jnp.zeros(span.shape, F32)
    for line_step in range(layout.lines):
        line = jnp.where(forward, line_step, layout.lines - 1 - line_step)
        entering = state
        for high_step in range(layout.highs):
            this = jnp.where(forward, high_step, layout.highs - 1 - high_step)
            entering = jnp.where(this == high, state, entering)
            peer = lax.rem(this + layout.highs - layout.middle, layout.highs)
            state = stride * state + totals_ref[peer, line]
        for step in range(layout.lows):
            low = jnp.where(forward, step, layout.lows - 1 - step)
            at = layout.slot(line, low)
            carried_ref[at] = entering
            entering = span * entering + ends_ref[at]


def carry_kernel(
    both_ref, rate_ref, carried_ref, out_hbm, grad_hbm, out_ref, grad_ref, sems
):
    positions, width = out_ref.shape
    states = rate_ref.shape[0]
    tiles = positions // SUB

    def part_copies(part):
        lanes = pl.ds(pl.multiple_of(part * 2 * LANES, 2 * LANES), 2 * LANES)
        return [
            pltpu.make_async_copy(ref.at[:, lanes], hbm.at[:, lanes], sems.at[side, part])
            for side, (hbm, ref) in enumerate(((out_hbm, out_ref), (grad_hbm, grad_ref)))
        ]

    def column(c, _):
        lanes = pl.ds(pl.multiple_of(c * LANES, LANES), LANES)
        decay_table = jnp.exp(-rate_ref[:, lanes] * float(SUB))
        decay = [row_of(decay_table, n) for n in range(states)]
        rows = pl.ds(pl.multiple_of(c * states, states), states)
        for side, result in enumerate((out_ref, grad_ref)):
            local_ref = both_ref.at[side]
            carried = carried_ref[side, rows, :]
            terms = [
                local_ref[pl.ds(positions + n * SUB, SUB), lanes] * row_of(carried, n)
                for n in range(states)
            ]
            for pair in range(tiles // 2):
                halves = []
                first = pair * 2 * SUB if side == 0 else positions - (pair + 1) * 2 * SUB
                for half in range(2):
                    if pair or half:
                        terms = [decay[n] * terms[n] for n in range(states)]
                    start = first + (half if side == 0 else 1 - half) * SUB
                    local = local_ref[pl.ds(start, SUB), lanes]
                    halves.append(added(terms) + local)
                if side:
                    halves.reverse()
                both = jnp.concatenate(halves, axis=0)
                result[first : first + 2 * SUB, lanes] = both.astype(result.dtype)
        return 0

    def both_columns(part, _):
        lax.fori_loop(2 * part, 2 * part + 2, column, 0)
        for copy in part_copies(part):
            copy.start()
        return 0

    lax.fori_loop(0, width // (2 * LANES), both_columns, 0)
    for part in range(width // (2 * LANES)):
        for copy in part_copies(part):
            copy.wait()


def vmem(mib):
    return pltpu.CompilerParams(vmem_limit_bytes=mib << 20)


def shards(signal, cotangent, decay_rate, residue, skip_gain):
    positions, channels = signal.shape
    states = decay_rate.shape[0]
    columns = channels // LANES
    devices = lax.axis_size("seq")
    anywhere = pl.BlockSpec(memory_space=pl.ANY)
    in_hbm = pl.BlockSpec(memory_space=pltpu.HBM)
    in_vmem = pl.BlockSpec(memory_space=pltpu.VMEM)
    elements = positions * channels * states
    whole = pltpu.VMEM((positions, channels), signal.dtype)
    turned = pltpu.VMEM(((states + 1) * columns, LANES), F32)
    copy_sems = pltpu.SemaphoreType.DMA((2, columns // 2))

    ends = pl.pallas_call(
        ends_kernel,
        in_specs=[in_hbm] * 3,
        out_specs=in_vmem,
        out_shape=jax.ShapeDtypeStruct((2, columns * states, LANES), F32),
        scratch_shapes=[
            whole,
            whole,
            pltpu.VMEM(decay_rate.shape, F32),
            copy_sems,
            pltpu.SemaphoreType.DMA,
        ],
        compiler_params=vmem(56),
        name="ends",
    )(signal, cotangent, decay_rate)

    layout = Layout(devices)
    rows = 2 * columns * states // layout.members
    index = lax.axis_index("seq").astype(jnp.int32).reshape(1)
    in_smem = pl.BlockSpec(memory_space=pltpu.SMEM)

    def exchanged(x, groups):
        return lax.all_to_all(x, "seq", 0, 0, axis_index_groups=groups)

    gathered = exchanged(ends.reshape(layout.members, rows, LANES), layout.member_groups())
    rate_then, _ = lax.optimization_barrier((decay_rate, ends))
    span = jnp.exp(-float(positions) * rate_then).reshape(states, columns, LANES)
    span = span.swapaxes(0, 1).reshape(columns * states, LANES)
    weight = residue * jnp.sqrt(-jnp.expm1(-2.0 * rate_then))
    tables = jnp.concatenate([rate_then, weight, skip_gain.reshape(1, channels)], axis=0)
    span, tables = lax.optimization_barrier((span, tables))
    totals = pl.pallas_call(
        functools.partial(totals_kernel, layout),
        in_specs=[in_smem, in_vmem, in_vmem],
        out_specs=in_vmem,
        out_shape=jax.ShapeDtypeStruct((layout.highs, layout.lines, rows, LANES), F32),
        compiler_params=vmem(4),
        name="totals",
    )(index, gathered, span)
    peers = exchanged(totals, layout.peer_groups())

    depth = positions + states * SUB

    def within(is_forward, x, *other):
        return pl.pallas_call(
            functools.partial(within_kernel, is_forward),
            in_specs=[in_vmem] * (2 + len(other)),
            out_specs=in_vmem,
            out_shape=jax.ShapeDtypeStruct((2, depth, channels), F32),
            input_output_aliases={2: 0} if other else {},
            scratch_shapes=[
                pltpu.VMEM(((2 * SUB + 1) * columns, LANES), F32),
                turned,
                turned,
                pltpu.VMEM((columns + SUB, LANES), F32),
            ],
            cost_estimate=pl.CostEstimate(
                flops=6 * elements, bytes_accessed=6 * positions * channels, transcendentals=0
            ),
            compiler_params=vmem(8),
            name="within_forward" if is_forward else "within_backward",
        )(x, tables, *other)

    signal, _ = lax.optimization_barrier((signal, totals))
    half = within(True, signal)
    span, half = lax.optimization_barrier((span, half))

    carried = pl.pallas_call(
        functools.partial(relay_kernel, layout),
        in_specs=[in_smem] + [in_vmem] * 3,
        out_specs=in_vmem,
        out_shape=jax.ShapeDtypeStruct((layout.members, rows, LANES), F32),
        compiler_params=vmem(4),
        name="relay",
    )(index, gathered, peers, span)
    cotangent, _ = lax.optimization_barrier((cotangent, carried))
    both = within(False, cotangent, half)
    returned = exchanged(carried, layout.member_groups())
    returned = returned.reshape(2, columns * states, LANES)

    return pl.pallas_call(
        carry_kernel,
        in_specs=[in_vmem] * 3,
        out_specs=[in_hbm] * 2,
        out_shape=[jax.ShapeDtypeStruct(signal.shape, signal.dtype)] * 2,
        scratch_shapes=[whole, whole, copy_sems],
        compiler_params=vmem(8),
        name="carry",
    )(both, decay_rate, returned)


def solution(mesh):
    in_specs = (P("seq", "chan"), P("seq", "chan"), P(None, "chan"), P(None, "chan"), P("chan"))
    out_specs = (P("seq", "chan"), P("seq", "chan"))
    return jax.shard_map(
        lambda *arrays: tuple(shards(*arrays)),
        mesh=mesh,
        in_specs=in_specs,
        out_specs=out_specs,
        check_vma=False,
    )
```
